32 devices in a mesh: dp: 16 (over z, y, x), tensor: 2 (over core).
Axes of the slice: x: 2, y: 2, z: 4, core: 2. Of those that a mesh axis runs over, the one named last changes fastest.
Arguments:
- tokens: bfloat16 [4096, 2048], P(('dp', 'tensor')), may hold values from -6 to 6
- cotangent: bfloat16 [4096, 2048], P(('dp', 'tensor')), may hold values from -6 to 6
- weight_qkv: bfloat16 [2048, 4096], P('dp', 'tensor'), may hold values from -0.125 to 0.125
- weight_out: bfloat16 [2048, 2048], P('tensor', 'dp'), may hold values from -1 to 1
- weight_gate_up: bfloat16 [2048, 12288], P('dp', 'tensor'), may hold values from -0.125 to 0.125
- weight_down: bfloat16 [6144, 2048], P('tensor', 'dp'), may hold values from -0.078125 to 0.078125
- norm_gains: bfloat16 [2, 2048], replicated, may hold values from 0.5 to 1.5
- head_gains: bfloat16 [2, 128], replicated, may hold values from 0.099609375 to 1.8984375
- first_qkv: float32 [2048, 4096], P('dp', 'tensor')
- second_qkv: float32 [2048, 4096], P('dp', 'tensor')
- first_out: float32 [2048, 2048], P('tensor', 'dp')
- second_out: float32 [2048, 2048], P('tensor', 'dp')
- first_gate_up: float32 [2048, 12288], P('dp', 'tensor')
- second_gate_up: float32 [2048, 12288], P('dp', 'tensor')
- first_down: float32 [6144, 2048], P('tensor', 'dp')
- second_down: float32 [6144, 2048], P('tensor', 'dp')
- first_norm: float32 [2, 2048], replicated
- second_norm: float32 [2, 2048], replicated
- first_head: float32 [2, 128], replicated
- second_head: float32 [2, 128], replicated
Outputs:
- output: bfloat16 [4096, 2048], P(('dp', 'tensor'))
- input_grad: float32 [4096, 2048], P(('dp', 'tensor'))
- grad_qkv: float32 [2048, 4096], P('dp', 'tensor')
- moment_one_qkv: float32 [2048, 4096], P('dp', 'tensor')
- moment_two_qkv: float32 [2048, 4096], P('dp', 'tensor')
- update_qkv: float32 [2048, 4096], P('dp', 'tensor')
- grad_out: float32 [2048, 2048], P('tensor', 'dp')
- moment_one_out: float32 [2048, 2048], P('tensor', 'dp')
- moment_two_out: float32 [2048, 2048], P('tensor', 'dp')
- update_out: float32 [2048, 2048], P('tensor', 'dp')
- grad_gate_up: float32 [2048, 12288], P('dp', 'tensor')
- moment_one_gate_up: float32 [2048, 12288], P('dp', 'tensor')
- moment_two_gate_up: float32 [2048, 12288], P('dp', 'tensor')
- update_gate_up: float32 [2048, 12288], P('dp', 'tensor')
- grad_down: float32 [6144, 2048], P('tensor', 'dp')
- moment_one_down: float32 [6144, 2048], P('tensor', 'dp')
- moment_two_down: float32 [6144, 2048], P('tensor', 'dp')
- update_down: float32 [6144, 2048], P('tensor', 'dp')
- grad_norm: float32 [2, 2048], replicated
- moment_one_norm: float32 [2, 2048], replicated
- moment_two_norm: float32 [2, 2048], replicated
- update_norm: float32 [2, 2048], replicated
- grad_head: float32 [2, 128], replicated
- moment_one_head: float32 [2, 128], replicated
- moment_two_head: float32 [2, 128], replicated
- update_head: float32 [2, 128], replicated
The draws below stay inside these ranges and needn't reach their ends.
All inputs are finite; a program needn't handle non-finite values.
Results may differ from the reference program's by a relative error of at most 0.015.
Values may be sent and summed in bfloat16 or wider, within the bound.
No kernel may reach another device: no remote copies, remote signals or barrier semaphores. Data moves between devices by JAX's collectives and lax.ppermute only.
A program may use at most 256 MiB of HBM per device.

```python
import math
import jax
import jax.numpy as jnp
from jax import lax

D = 2048
QUERY_HEADS = 16
KEY_VALUE_HEADS = 8
HEAD_SIZE = 128
FF = 6144
SEQ = 256
STEP = 10
TOKENS = 4096
QKV = 4096
N_DP = 16
N_TENSOR = 2


def first_moment(key, array_shape, factor):
    spread = 0.111 * factor * math.sqrt(TOKENS)
    return jax.random.normal(key, array_shape, jnp.float32) * spread


def second_moment(key, array_shape, factor):
    spread = 0.0526 * factor * factor * TOKENS
    exponent = jax.random.uniform(key, array_shape, jnp.float32, math.log(0.25), math.log(4.0))
    return jnp.exp(exponent) * spread


def draw_first_qkv(key, part):
    return first_moment(jax.random.fold_in(key, 101), (D, QKV), 1.0)


def draw_second_qkv(key, part):
    return second_moment(jax.random.fold_in(key, 102), (D, QKV), 1.0)


def draw_first_out(key, part):
    return first_moment(jax.random.fold_in(key, 103), (QUERY_HEADS * HEAD_SIZE, D), 0.1)


def draw_second_out(key, part):
    return second_moment(jax.random.fold_in(key, 104), (QUERY_HEADS * HEAD_SIZE, D), 0.1)


def draw_first_gate_up(key, part):
    return first_moment(jax.random.fold_in(key, 105), (D, 2 * FF), 0.3)


def draw_second_gate_up(key, part):
    return second_moment(jax.random.fold_in(key, 106), (D, 2 * FF), 0.3)


def draw_first_down(key, part):
    return first_moment(jax.random.fold_in(key, 107), (FF, D), 0.5)


def draw_second_down(key, part):
    return second_moment(jax.random.fold_in(key, 108), (FF, D), 0.5)


def draw_first_norm(key, part):
    return first_moment(jax.random.fold_in(key, 109), (2, D), 2.0)


def draw_second_norm(key, part):
    return second_moment(jax.random.fold_in(key, 110), (2, D), 2.0)


def draw_first_head(key, part):
    return first_moment(jax.random.fold_in(key, 111), (2, HEAD_SIZE), 5.0)


def draw_second_head(key, part):
    return second_moment(jax.random.fold_in(key, 112), (2, HEAD_SIZE), 5.0)


def block_scale(own_key, shape, pieces, least, high):
    def one(axis_at, shards_of):
        heights = jax.random.uniform(jax.random.fold_in(jax.random.fold_in(own_key, 6), axis_at), (shards_of,), jnp.float32, least / len(pieces), high / len(pieces))
        return jnp.repeat(jnp.exp(heights), shape[axis_at] // shards_of).reshape((-1,) + (1,) * (len(shape) - axis_at - 1))

    loudness = one(*pieces[0])
    for cut in pieces[1:]:
        loudness = loudness * one(*cut)
    return loudness


def gaussian(own_key, extent, scale, most, split=(), kind=jnp.bfloat16):
    drawn = jax.random.normal(own_key, extent, jnp.float32) * scale
    if len(split) > 0:
        drawn = block_scale(own_key, extent, split, -0.22, 0.18) * drawn
    return jnp.clip(drawn, min=-most, max=most).astype(kind)


def setup_inputs(seed: int = 0) -> dict:
    keys = jax.random.split(jax.random.key(seed), 21)
    return {
        "tokens": gaussian(keys[0], (TOKENS, D), 1.0, 6.0, ((0, 32),)),
        "cotangent": gaussian(keys[1], (TOKENS, D), 1.0, 6.0, ((0, 32),)),
        "weight_qkv": gaussian(keys[2], (D, QKV), D ** -0.5, 0.125, ((0, 16), (1, 2))),
        "weight_out": gaussian(keys[3], (QUERY_HEADS * HEAD_SIZE, D), (max(QUERY_HEADS * HEAD_SIZE // 64, 1)) ** -0.5, 1.0, ((0, 2), (1, 16))),
        "weight_gate_up": gaussian(keys[4], (D, 2 * FF), D ** -0.5, 0.125, ((0, 16), (1, 2))),
        "weight_down": gaussian(keys[5], (FF, D), FF ** -0.5, 0.078125, ((0, 2), (1, 16))),
        "norm_gains": jnp.clip(1.0 + 0.1 * jax.random.normal(keys[6], (2, D), jnp.float32), 0.5, 1.5).astype(jnp.bfloat16),
        "head_gains": jnp.clip(1.0 + 0.18 * jax.random.normal(keys[7], (2, HEAD_SIZE), jnp.float32), 0.099609375, 1.8984375).astype(jnp.bfloat16),
        "first_qkv": draw_first_qkv(jax.random.fold_in(keys[20], 71), 0),
        "second_qkv": draw_second_qkv(jax.random.fold_in(keys[20], 71), 0),
        "first_out": draw_first_out(jax.random.fold_in(keys[20], 71), 0),
        "second_out": draw_second_out(jax.random.fold_in(keys[20], 71), 0),
        "first_gate_up": draw_first_gate_up(jax.random.fold_in(keys[20], 71), 0),
        "second_gate_up": draw_second_gate_up(jax.random.fold_in(keys[20], 71), 0),
        "first_down": draw_first_down(jax.random.fold_in(keys[20], 71), 0),
        "second_down": draw_second_down(jax.random.fold_in(keys[20], 71), 0),
        "first_norm": draw_first_norm(jax.random.fold_in(keys[20], 71), 0),
        "second_norm": draw_second_norm(jax.random.fold_in(keys[20], 71), 0),
        "first_head": draw_first_head(jax.random.fold_in(keys[20], 71), 0),
        "second_head": draw_second_head(jax.random.fold_in(keys[20], 71), 0),
    }


@jax.custom_vjp
def low(v):
    return lax.optimization_barrier(v.astype(jnp.bfloat16)).astype(jnp.float32)

@jax.custom_vjp
def low_back(v):
    return v

def low_keep(v):
    return (low(v), None)

def low_pass(kept, grad):
    return (grad,)

def back_keep(v):
    return (v, None)

def back_low(kept, grad):
    return (low(grad),)
low.defvjp(low_keep, low_pass)
low_back.defvjp(back_keep, back_low)
norm_eps = 1e-06
rope_base = 1000000.0
beta_one = 0.9
beta_two = 0.95
adam_eps = 1e-08
learn_rate = 0.01
weight_decay = 0.1

def product(left, right):
    return jnp.dot(left, right, precision=lax.Precision.HIGHEST, preferred_element_type=jnp.float32)

def rms_scale(values):
    return lax.rsqrt(lax.optimization_barrier(jnp.mean(values * values, axis=-1, keepdims=True)) + norm_eps)

def rope_tables(sequence_length, width):
    places = jnp.arange(sequence_length, dtype=jnp.float32)[:, None]
    index = jnp.arange(width // 2, dtype=jnp.float32)[None, :]
    angles = places * jnp.power(rope_base, -2.0 * index / width)
    return (jnp.cos(angles)[:, None, :], jnp.sin(angles)[:, None, :])

def rotary(values, cosine, sine_table):
    half_width = values.shape[-1] // 2
    first_half = values[..., :half_width]
    second_half = values[..., half_width:]
    return jnp.concatenate([first_half * cosine - second_half * sine_table, second_half * cosine + first_half * sine_table], axis=-1)

def block_forward(inputs, weight_qkv, weight_out, weight_gate_up, weight_down, norm_gains, head_gains):
    sequence_length = inputs.shape[0]
    query_columns = QUERY_HEADS // N_TENSOR * HEAD_SIZE
    key_value_columns = KEY_VALUE_HEADS // N_TENSOR * HEAD_SIZE
    normed_one = low(inputs * rms_scale(inputs) * norm_gains[0])
    projected_rows = low_back(product(normed_one, weight_qkv)).reshape(sequence_length, N_TENSOR, query_columns + 2 * key_value_columns)
    queries = projected_rows[:, :, :query_columns].reshape(sequence_length, QUERY_HEADS, HEAD_SIZE)
    unrotated_keys = projected_rows[:, :, query_columns:query_columns + key_value_columns].reshape(sequence_length, KEY_VALUE_HEADS, HEAD_SIZE)
    unscaled_values = projected_rows[:, :, query_columns + key_value_columns:].reshape(sequence_length, KEY_VALUE_HEADS, HEAD_SIZE)
    cosine, sine_table = rope_tables(sequence_length, HEAD_SIZE)
    q_rot = low(rotary(queries * rms_scale(queries) * head_gains[0], cosine, sine_table))
    k_rot = low(rotary(unrotated_keys * rms_scale(unrotated_keys) * head_gains[1], cosine, sine_table))
    values = low(unscaled_values)
    query_group_width = QUERY_HEADS // KEY_VALUE_HEADS
    k_rot = jnp.repeat(k_rot, query_group_width, axis=1)
    values = jnp.repeat(values, query_group_width, axis=1)
    scores = low_back(jnp.einsum('qhd,khd->hqk', q_rot, k_rot, precision=lax.Precision.HIGHEST)) / math.sqrt(HEAD_SIZE)
    causal = jnp.arange(sequence_length)[:, None] >= jnp.arange(sequence_length)[None, :]
    scores = jnp.where(causal[None], scores, -jnp.inf)
    attn_probs = jax.nn.softmax(scores, axis=-1)
    attended = jnp.einsum('hqk,khd->qhd', low(attn_probs), values, precision=lax.Precision.HIGHEST).reshape(sequence_length, QUERY_HEADS * HEAD_SIZE)
    attended = low_back(low(attended))
    middle = inputs + low_back(product(attended, weight_out))
    normed_two = low(middle * rms_scale(middle) * norm_gains[1])
    gate_up = low_back(product(normed_two, weight_gate_up)).reshape(sequence_length, N_TENSOR, 2, FF // N_TENSOR)
    gate_part = gate_up[:, :, 0].reshape(sequence_length, FF)
    up_part = gate_up[:, :, 1].reshape(sequence_length, FF)
    activation = low(jax.nn.silu(gate_part) * up_part)
    return middle + low_back(product(activation, weight_down))

def adamw_step(weight, gradient, old_first, old_second, step_value, decay):
    moment_one = beta_one * old_first + (1.0 - beta_one) * gradient
    moment_two = beta_two * old_second + (1.0 - beta_two) * gradient * gradient
    fix_one = 1.0 - jnp.power(beta_one, step_value)
    fix_two = 1.0 - jnp.power(beta_two, step_value)
    update = -learn_rate * (moment_one / fix_one / (jnp.sqrt(moment_two / fix_two) + adam_eps) + decay * weight)
    return (gradient, moment_one, moment_two, update)

def reference(tokens, cotangent, weight_qkv, weight_out, weight_gate_up, weight_down, norm_gains, head_gains, first_qkv, second_qkv, first_out, second_out, first_gate_up, second_gate_up, first_down, second_down, first_norm, second_norm, first_head, second_head):
    masters = (weight_qkv.astype(jnp.float32), weight_out.astype(jnp.float32), weight_gate_up.astype(jnp.float32), weight_down.astype(jnp.float32), norm_gains.astype(jnp.float32), head_gains.astype(jnp.float32))
    inputs = tokens.astype(jnp.float32).reshape(N_DP, SEQ, D)
    step_forward = jax.checkpoint(block_forward)

    def forward(batch, *weights):
        return lax.map(lambda sequence: step_forward(sequence, *weights), batch)
    result, pullback = jax.vjp(forward, inputs, *masters)
    gradients = pullback(cotangent.astype(jnp.float32).reshape(N_DP, SEQ, D))
    step_value = jnp.float32(STEP)
    output = result.reshape(TOKENS, D).astype(jnp.bfloat16)
    input_grad = gradients[0].reshape(TOKENS, D)
    qkv_new = adamw_step(masters[0], gradients[1], first_qkv, second_qkv, step_value, weight_decay)
    out_new = adamw_step(masters[1], gradients[2], first_out, second_out, step_value, weight_decay)
    gate_new = adamw_step(masters[2], gradients[3], first_gate_up, second_gate_up, step_value, weight_decay)
    down_new = adamw_step(masters[3], gradients[4], first_down, second_down, step_value, weight_decay)
    norm_new = adamw_step(masters[4], gradients[5], first_norm, second_norm, step_value, 0.0)
    head_new = adamw_step(masters[5], gradients[6], first_head, second_head, step_value, 0.0)
    return (output, input_grad, qkv_new[0], qkv_new[1], qkv_new[2], qkv_new[3], out_new[0], out_new[1], out_new[2], out_new[3], gate_new[0], gate_new[1], gate_new[2], gate_new[3], down_new[0], down_new[1], down_new[2], down_new[3], norm_new[0], norm_new[1], norm_new[2], norm_new[3], head_new[0], head_new[1], head_new[2], head_new[3])
```

```python
import functools
import math

import jax
import jax.numpy as jnp
from jax import lax
from jax.experimental import pallas as pl
from jax.experimental.pallas import tpu as pltpu
from jax.sharding import Mesh
from jax.sharding import PartitionSpec as P

HEAD_SIZE = 128
STEP = 10

norm_eps = 1e-06
rope_base = 1000000.0
beta_one = 0.9
beta_two = 0.95
adam_eps = 1e-08
learn_rate = 0.01
weight_decay = 0.1

bf16 = jnp.bfloat16
f32 = jnp.float32

SWAP = [(0, 1), (1, 0)]


def dot(left, right):
    return jnp.dot(left, right, preferred_element_type=f32)


def dot_tn(left, right):
    return lax.dot_general(left, right, (((0,), (0,)), ((), ())), preferred_element_type=f32)


def dot_nt(left, right):
    return lax.dot_general(left, right, (((1,), (1,)), ((), ())), preferred_element_type=f32)


def swap(value, axis):
    return lax.ppermute(value, axis, SWAP)


def rms_scale(values):
    return lax.rsqrt(jnp.mean(values * values, axis=-1, keepdims=True) + norm_eps)


def norm_back(upstream, values, scale, gain):
    weighted = upstream * gain
    normed = values * scale
    grad_values = scale * (weighted - normed * jnp.mean(weighted * normed, axis=-1, keepdims=True))
    grad_gain = jnp.sum((upstream * normed).reshape(-1, values.shape[-1]), axis=0)
    return (grad_values, grad_gain)


def adamw_step(weight, gradient, old_first, old_second, step_value, decay):
    moment_one = beta_one * old_first + (1.0 - beta_one) * gradient
    moment_two = beta_two * old_second + (1.0 - beta_two) * gradient * gradient
    fix_one = 1.0 - jnp.power(beta_one, step_value)
    fix_two = 1.0 - jnp.power(beta_two, step_value)
    update = -learn_rate * (
        moment_one / fix_one / (jnp.sqrt(moment_two / fix_two) + adam_eps) + decay * weight
    )
    return (gradient, moment_one, moment_two, update)


def vmem_call(kernel, out_shape, *args, name, flops=0):
    size = sum(math.prod(a.shape) * a.dtype.itemsize for a in (*args, *jax.tree.leaves(out_shape)))
    return pl.pallas_call(
        kernel,
        in_specs=[pl.BlockSpec(memory_space=pltpu.SMEM)] + [pl.BlockSpec(memory_space=pltpu.VMEM)] * (len(args) - 1),
        out_specs=jax.tree.map(lambda _: pl.BlockSpec(memory_space=pltpu.VMEM), out_shape),
        out_shape=out_shape,
        cost_estimate=pl.CostEstimate(flops=flops, bytes_accessed=size, transcendentals=0),
        compiler_params=pltpu.CompilerParams(vmem_limit_bytes=40 * 1024 * 1024),
        name=name,
    )(*args)


def shape(rows, columns, dtype):
    return jax.ShapeDtypeStruct((rows, columns), dtype)


def moves(place_ref, width):
    block = width // 16
    zh, x = place_ref[0], place_ref[1]
    for i in range(16):
        xr, zr, j = i // 8, (i // 4) % 2, i % 4
        natural = ((zr + zh - 2 * zr * zh) * 4 + j) * 2 + (xr + x - 2 * xr * x)
        yield pl.ds(i * block, block), pl.ds(pl.multiple_of(natural * block, block), block)


def start_kernel(place, tokens, cotangent, gains, own_tokens, normed, own_cotangent, own_gains):
    values = tokens[...].astype(f32)
    scale = rms_scale(values)
    for own, natural in moves(place, tokens.shape[1]):
        part = tokens[:, natural]
        gain = gains[:, natural]
        own_tokens[:, own] = part
        own_gains[:, own] = gain
        normed[:, own] = (part.astype(f32) * scale * gain[0:1]).astype(bf16)
        own_cotangent[:, own] = cotangent[:, natural]


def middle_kernel(place, base, near, far, tokens, gains, middle, normed):
    value = tokens[...].astype(f32) + (base[...] + near[...].astype(f32) + far[...].astype(f32))
    middle[...] = value
    normed[...] = (value * rms_scale(value) * gains[1:2]).astype(bf16)


def output_kernel(place, base, near, far, middle, output):
    for own, natural in moves(place, middle.shape[1]):
        added = base[:, own] + near[:, own].astype(f32) + far[:, own].astype(f32)
        output[:, natural] = (middle[:, own] + added).astype(bf16)


def back_two_kernel(place, base, near, far, middle, cotangent, gains, grad_middle, branch, dgain):
    upstream = base[...] + near[...].astype(f32) + far[...].astype(f32)
    value = middle[...]
    part, gain_part = norm_back(upstream, value, rms_scale(value), gains[1:2])
    grad = cotangent[...].astype(f32) + part
    grad_middle[...] = grad
    branch[...] = grad.astype(bf16)
    dgain[...] = gain_part[None]


def back_one_kernel(place, base, near, far, tokens, grad_middle, gains, dgain_two, input_grad, dgain):
    value = tokens[...].astype(f32)
    scale = rms_scale(value)
    upstream = base[...] + near[...].astype(f32) + far[...].astype(f32)
    normed = value * scale
    weighted = upstream * gains[0:1]
    mean = jnp.mean(weighted * normed, axis=-1, keepdims=True)
    for own, natural in moves(place, tokens.shape[1]):
        raised = base[:, own] + near[:, own].astype(f32) + far[:, own].astype(f32)
        unit = tokens[:, own].astype(f32) * scale
        grad = scale * (raised * gains[0:1, own] - unit * mean)
        input_grad[:, natural] = grad_middle[:, own] + grad
        dgain[0:1, natural] = jnp.sum(raised * unit, axis=0, keepdims=True)
        dgain[1:2, natural] = dgain_two[:, own]


def join_kernel(count, *refs):
    parts, out, done = refs[:count], refs[count], refs[count + 1]
    copies, at = [], 0
    for i, part in enumerate(parts):
        rows = part.shape[0]
        copies.append(pltpu.make_async_copy(part, out.at[pl.ds(at, rows)], done.at[i]))
        at += rows
    for copy in copies:
        copy.start()
    for copy in copies:
        copy.wait()


def join(*parts):
    total = shape(sum(p.shape[0] for p in parts), parts[0].shape[1], parts[0].dtype)
    size = 2 * total.shape[0] * total.shape[1] * total.dtype.itemsize
    return pl.pallas_call(
        functools.partial(join_kernel, len(parts)),
        in_specs=[pl.BlockSpec(memory_space=pl.ANY)] * len(parts),
        out_specs=pl.BlockSpec(memory_space=pltpu.VMEM),
        out_shape=total,
        scratch_shapes=[pltpu.SemaphoreType.DMA((len(parts),))],
        cost_estimate=pl.CostEstimate(flops=0, bytes_accessed=size, transcendentals=0),
        compiler_params=pltpu.CompilerParams(vmem_limit_bytes=16 * 1024 * 1024),
        name="join",
    )(*parts)


def gather_rows(value):
    over_zl = swap(value, "zl")
    over_y = swap(value, "y")
    over_both = swap(over_zl, "y")
    half = join(value, over_y, over_zl, over_both)
    return join(half, swap(half, "c"))


def sum_rows(left, right_t):
    half = left.shape[0] // 2
    rows = half // 4
    other = dot_nt(left[half:], right_t).astype(bf16)
    mine = dot_nt(left[:half], right_t) + swap(other, "c").astype(f32)
    block = lambda i: mine[i * rows : (i + 1) * rows]
    both = swap(block(3).astype(bf16), "y")
    near = swap(block(1).astype(bf16), "y")
    far = swap((block(2) + both.astype(f32)).astype(bf16), "zl")
    return block(0), near, far


def pack_attention_kernel(wide_q, wide_kv, qkv, out, packed):
    for j in range(4):
        packed[j, :, :wide_q] = qkv[:, j * wide_q : (j + 1) * wide_q]
        for part in range(2):
            at = 4 * (wide_q + part * wide_kv) + j * wide_kv
            to = wide_q + part * wide_kv
            packed[j, :, to : to + wide_kv] = qkv[:, at : at + wide_kv]
        turned = out[j * wide_q : (j + 1) * wide_q, :].astype(f32).T
        packed[j, :, wide_q + 2 * wide_kv :] = turned.astype(bf16)


def pack_attention(qkv, out, wide_q, wide_kv):
    depth = qkv.shape[0]
    packed = jax.ShapeDtypeStruct((4, depth, 2 * wide_q + 2 * wide_kv), bf16)
    return pl.pallas_call(
        functools.partial(pack_attention_kernel, wide_q, wide_kv),
        out_shape=packed,
        compiler_params=pltpu.CompilerParams(vmem_limit_bytes=40 * 1024 * 1024),
        name="pack_attention",
    )(qkv, out)


def pack_columns_kernel(first, second, packed):
    wide = first.shape[1]
    packed[0, :, :wide] = first[...]
    packed[0, :, wide:] = second[...]


def pack_columns(array, wide):
    depth = array.shape[0]
    return pl.pallas_call(
        pack_columns_kernel,
        grid=(4,),
        in_specs=[
            pl.BlockSpec((depth, wide), lambda j: (0, j)),
            pl.BlockSpec((depth, wide), lambda j: (0, j + 4)),
        ],
        out_specs=pl.BlockSpec((1, depth, 2 * wide), lambda j: (j, 0, 0)),
        out_shape=jax.ShapeDtypeStruct((4, depth, 2 * wide), bf16),
        compiler_params=pltpu.CompilerParams(vmem_limit_bytes=40 * 1024 * 1024),
        name="pack_columns",
    )(array, array)


def pack_turned_kernel(array, packed):
    packed[0] = array[...].astype(f32).T.astype(bf16)


def pack_turned(array, wide):
    depth = array.shape[1]
    return pl.pallas_call(
        pack_turned_kernel,
        grid=(4,),
        in_specs=[pl.BlockSpec((wide, depth), lambda j: (j, 0))],
        out_specs=pl.BlockSpec((1, depth, wide), lambda j: (j, 0, 0)),
        out_shape=jax.ShapeDtypeStruct((4, depth, wide), bf16),
        compiler_params=pltpu.CompilerParams(vmem_limit_bytes=40 * 1024 * 1024),
        name="pack_turned",
    )(array)


def exchange(pieces):
    return lax.all_to_all(pieces, ("zl", "y"), 0, 0, tiled=True)


def gather_weight(pieces, rest):
    mine = exchange(pieces)
    if rest > 1:
        mine = lax.all_gather(mine, "r", axis=1, tiled=True)
    mine = mine.reshape(-1, mine.shape[-1])
    far = swap(mine, "zh")
    return jnp.concatenate([mine, far, swap(mine, "x"), swap(far, "x")], axis=0)


def scatter_grad(left, right, rest):
    width = left.shape[1]
    over_x = swap(dot_tn(left[:, width // 2 :], right).astype(bf16), "x")
    near = dot_tn(left[:, : width // 2], right) + over_x.astype(f32)
    far = swap(near[width // 4 :].astype(bf16), "zh")
    mine = (near[: width // 4] + far.astype(f32)).astype(bf16)
    mine = mine.reshape(4, width // 16, -1)
    if rest > 1:
        mine = lax.psum_scatter(mine, "r", scatter_dimension=1, tiled=True)
    return exchange(mine)


fix_one = 1.0 - beta_one**STEP
fix_two = 1.0 - beta_two**STEP


def adam_store(refs, at, gradient):
    weight, first, second, grad_out, one_out, two_out, update_out = refs
    moment_one = beta_one * first[at] + (1.0 - beta_one) * gradient
    moment_two = beta_two * second[at] + (1.0 - beta_two) * gradient * gradient
    ratio = moment_one * (1.0 / fix_one) / (jnp.sqrt(moment_two * (1.0 / fix_two)) + adam_eps)
    grad_out[at] = gradient
    one_out[at] = moment_one
    two_out[at] = moment_two
    update_out[at] = -learn_rate * (ratio + weight_decay * weight[at].astype(f32))


def adam_qkv_kernel(wide_q, wide_kv, got, *refs):
    for j in range(4):
        at, to = 0, 0
        for wide in (wide_q, wide_kv, wide_kv):
            part = got[j, :, at : at + wide].astype(f32)
            adam_store(refs, (slice(None), slice(to + j * wide, to + (j + 1) * wide)), part)
            at += wide
            to += 4 * wide


def adam_columns_kernel(got, *refs):
    adam_store(refs, (slice(None), slice(None)), got[0].astype(f32))


def adam_turned_kernel(got, *refs):
    adam_store(refs, (slice(None), slice(None)), got[0].astype(f32).T)


def adam(kernel, grid, got, got_spec, spec, weight, first, second, name):
    out = jax.ShapeDtypeStruct(weight.shape, f32)
    size = math.prod(weight.shape) * 28
    return pl.pallas_call(
        kernel,
        grid=grid,
        in_specs=[got_spec, spec, spec, spec],
        out_specs=[spec] * 4,
        out_shape=[out] * 4,
        cost_estimate=pl.CostEstimate(flops=size // 2, bytes_accessed=size, transcendentals=0),
        compiler_params=pltpu.CompilerParams(vmem_limit_bytes=40 * 1024 * 1024),
        name=name,
    )(got, weight, first, second)


def adam_qkv(got, weight, first, second, wide_q, wide_kv):
    kernel = functools.partial(adam_qkv_kernel, wide_q, wide_kv)
    whole = lambda array: pl.BlockSpec(array.shape, lambda i: (0,) * array.ndim)
    return adam(kernel, (1,), got, whole(got), whole(weight), weight, first, second, "adam_qkv")


def adam_columns(got, weight, first, second, wide):
    depth, columns = weight.shape
    got_spec = pl.BlockSpec((1, depth, wide), lambda b: (b % 4, 0, b // 4))
    spec = pl.BlockSpec((depth, wide), lambda b: (0, b))
    grid = (columns // wide,)
    return adam(adam_columns_kernel, grid, got, got_spec, spec, weight, first, second, "adam_columns")


def adam_turned(got, weight, first, second, wide):
    depth = weight.shape[1]
    got_spec = pl.BlockSpec((1, depth, wide), lambda j: (j, 0, 0))
    spec = pl.BlockSpec((wide, depth), lambda j: (j, 0))
    return adam(adam_turned_kernel, (4,), got, got_spec, spec, weight, first, second, "adam_turned")


def rope(v, cosine, sine):
    return v * cosine + pltpu.roll(v, HEAD_SIZE // 2, 1) * sine


def rope_back(v, cosine, sine):
    return v * cosine - pltpu.roll(v, HEAD_SIZE // 2, 1) * sine


def head_norm(v, gain, cosine, sine):
    scale = rms_scale(v)
    return scale, rope(v * scale * gain, cosine, sine).astype(bf16)


def probabilities(q_rot, k_rot, shift):
    length = q_rot.shape[0]
    scores = dot_nt(q_rot, k_rot) * (1.0 / math.sqrt(HEAD_SIZE))
    rows = lax.broadcasted_iota(jnp.int32, (length, length), 0)
    cols = lax.broadcasted_iota(jnp.int32, (length, length), 1)
    place_q = jnp.where(rows >= length - shift, rows + shift - length, rows + shift)
    place_k = jnp.where(cols >= length - shift, cols + shift - length, cols + shift)
    scores = jnp.where(place_q >= place_k, scores, -jnp.inf)
    terms = jnp.exp(scores - jnp.max(scores, axis=-1, keepdims=True))
    return terms / jnp.sum(terms, axis=-1, keepdims=True)


def attend_kernel(heads_q, heads_kv, shift_ref, proj_ref, cos_ref, sin_ref, gain_ref, out_ref):
    half, columns = proj_ref.shape[2:]
    cosine, sine = cos_ref[...], sin_ref[...]
    shift = shift_ref[0]
    group = heads_q // heads_kv

    def column(i):
        return proj_ref[:, 0, :, i * HEAD_SIZE : (i + 1) * HEAD_SIZE].reshape(2 * half, HEAD_SIZE)

    for kv in range(heads_kv):
        _, k_rot = head_norm(column(heads_q + kv), gain_ref[1:2, :], cosine, sine)
        values = column(heads_q + heads_kv + kv).astype(bf16)
        for h in range(kv * group, (kv + 1) * group):
            _, q_rot = head_norm(column(h), gain_ref[0:1, :], cosine, sine)
            probs = probabilities(q_rot, k_rot, shift)
            out = dot(probs.astype(bf16), values).astype(bf16)
            out_ref[:, 0, :, h * HEAD_SIZE : (h + 1) * HEAD_SIZE] = out.reshape(2, half, HEAD_SIZE)


def attend_back_kernel(
    heads_q, heads_kv, shift_ref, proj_ref, datt_ref, cos_ref, sin_ref, gain_ref, out_ref, dgain_ref
):
    half, columns = proj_ref.shape[2:]
    cosine, sine = cos_ref[...], sin_ref[...]
    shift = shift_ref[0]
    group = heads_q // heads_kv
    inv_root = 1.0 / math.sqrt(HEAD_SIZE)

    @pl.when(pl.program_id(0) == 0)
    def _():
        dgain_ref[...] = jnp.zeros_like(dgain_ref)

    def column(ref, i):
        return ref[:, 0, :, i * HEAD_SIZE : (i + 1) * HEAD_SIZE].reshape(2 * half, HEAD_SIZE)

    def store(i, value):
        value = value.astype(bf16).reshape(2, half, HEAD_SIZE)
        out_ref[:, 0, :, i * HEAD_SIZE : (i + 1) * HEAD_SIZE] = value

    q_gain, k_gain = gain_ref[0:1, :], gain_ref[1:2, :]
    dgain_q = jnp.zeros((1, HEAD_SIZE), f32)
    dgain_k = jnp.zeros((1, HEAD_SIZE), f32)
    for kv in range(heads_kv):
        key = column(proj_ref, heads_q + kv)
        k_scale, k_rot = head_norm(key, k_gain, cosine, sine)
        values = column(proj_ref, heads_q + heads_kv + kv).astype(bf16)
        grad_values = jnp.zeros((2 * half, HEAD_SIZE), f32)
        grad_keys = jnp.zeros((2 * half, HEAD_SIZE), f32)
        for h in range(kv * group, (kv + 1) * group):
            query = column(proj_ref, h)
            d_att = column(datt_ref, h)
            q_scale, q_rot = head_norm(query, q_gain, cosine, sine)
            probs = probabilities(q_rot, k_rot, shift)
            grad_probs = dot_nt(d_att, values)
            row_delta = jnp.sum(probs * grad_probs, axis=-1, keepdims=True)
            d_scores = (probs * (grad_probs - row_delta) * inv_root).astype(bf16)
            grad_values += dot_tn(probs.astype(bf16), d_att)
            grad_keys += dot_tn(d_scores, q_rot)
            upstream = rope_back(dot(d_scores, k_rot), cosine, sine)
            raw, gain_part = norm_back(upstream, query, q_scale, q_gain)
            dgain_q += gain_part[None]
            store(h, raw)
        raw, gain_part = norm_back(rope_back(grad_keys, cosine, sine), key, k_scale, k_gain)
        dgain_k += gain_part[None]
        store(heads_q + kv, raw)
        store(heads_q + heads_kv + kv, grad_values)
    dgain_ref[0:1, :] += dgain_q
    dgain_ref[1:2, :] += dgain_k


def block_spec(half, columns):
    return pl.BlockSpec((2, 1, half, columns), lambda s: (0, s, 0, 0))


def whole_spec(array):
    return pl.BlockSpec(array.shape, lambda s: (0,) * array.ndim)


def attend(proj, shift, cosine, sine, gains, heads_q, heads_kv):
    _, seqs, half, columns = proj.shape
    return pl.pallas_call(
        functools.partial(attend_kernel, heads_q, heads_kv),
        grid=(seqs,),
        in_specs=[
            pl.BlockSpec(memory_space=pltpu.SMEM),
            block_spec(half, columns),
            whole_spec(cosine),
            whole_spec(sine),
            whole_spec(gains),
        ],
        out_specs=block_spec(half, heads_q * HEAD_SIZE),
        out_shape=jax.ShapeDtypeStruct((2, seqs, half, heads_q * HEAD_SIZE), bf16),
        compiler_params=pltpu.CompilerParams(vmem_limit_bytes=32 * 1024 * 1024),
        name="attend",
    )(shift, proj, cosine, sine, gains)


def attend_back(proj, d_att, shift, cosine, sine, gains, heads_q, heads_kv):
    _, seqs, half, columns = proj.shape
    return pl.pallas_call(
        functools.partial(attend_back_kernel, heads_q, heads_kv),
        grid=(seqs,),
        in_specs=[
            pl.BlockSpec(memory_space=pltpu.SMEM),
            block_spec(half, columns),
            block_spec(half, heads_q * HEAD_SIZE),
            whole_spec(cosine),
            whole_spec(sine),
            whole_spec(gains),
        ],
        out_specs=[block_spec(half, columns), pl.BlockSpec((2, HEAD_SIZE), lambda s: (0, 0))],
        out_shape=[
            jax.ShapeDtypeStruct((2, seqs, half, columns), bf16),
            jax.ShapeDtypeStruct((2, HEAD_SIZE), f32),
        ],
        compiler_params=pltpu.CompilerParams(vmem_limit_bytes=32 * 1024 * 1024),
        name="attend_back",
    )(shift, proj, d_att, cosine, sine, gains)


def shards(
    rest,
    tokens,
    cotangent,
    weight_qkv,
    weight_out,
    weight_gate_up,
    weight_down,
    norm_gains,
    head_gains,
    first_qkv,
    second_qkv,
    first_out,
    second_out,
    first_gate_up,
    second_gate_up,
    first_down,
    second_down,
    first_norm,
    second_norm,
    first_head,
    second_head,
):
    heads_q = weight_out.shape[0] // HEAD_SIZE // 4
    heads_kv = (weight_qkv.shape[1] // HEAD_SIZE - 4 * heads_q) // 2 // 4
    hidden = weight_down.shape[0] // 4
    wide_q, wide_kv = heads_q * HEAD_SIZE, heads_kv * HEAD_SIZE
    wide_qkv = wide_q + 2 * wide_kv
    half, width = tokens.shape
    head_rows = head_gains.astype(f32)
    place = jnp.stack([lax.axis_index("zh"), lax.axis_index("x")]).astype(jnp.int32)

    inputs, normed_own, own_cotangent, own_gains = vmem_call(
        start_kernel,
        [shape(half, width, bf16)] * 3 + [shape(2, width, f32)],
        place, tokens, cotangent, norm_gains.astype(f32),
        name="start",
    )
    attention = gather_weight(pack_attention(weight_qkv, weight_out, wide_q, wide_kv), rest)
    own_qkv, own_out = attention[:, :wide_qkv], attention[:, wide_qkv:]
    normed_one = gather_rows(normed_own)
    own_gate_up = gather_weight(pack_columns(weight_gate_up, hidden), rest)
    own_down = gather_weight(pack_turned(weight_down, hidden), rest)
    cotangent_all = gather_rows(own_cotangent)

    core = lax.axis_index("c")
    shift = (core * half).astype(jnp.int32)
    places = (jnp.arange(2 * half) + shift) % (2 * half)
    index = jnp.arange(HEAD_SIZE // 2, dtype=f32)[None, :]
    angles = places.astype(f32)[:, None] * jnp.power(rope_base, -2.0 * index / HEAD_SIZE)
    cosine = jnp.concatenate([jnp.cos(angles)] * 2, axis=1)
    sine = jnp.concatenate([-jnp.sin(angles), jnp.sin(angles)], axis=1)
    shift = shift.reshape(1)

    projected = dot(normed_one, own_qkv)
    projected = projected.reshape(2, 4, half, wide_qkv)
    attended = attend(projected, shift, cosine, sine, head_rows, heads_q, heads_kv)
    attended = attended.reshape(-1, wide_q)
    middle, normed_own = vmem_call(
        middle_kernel,
        [shape(half, width, f32), shape(half, width, bf16)],
        place, *sum_rows(attended, own_out), inputs, own_gains,
        name="middle",
    )

    normed_two = gather_rows(normed_own)
    gate_up = dot(normed_two, own_gate_up)
    gate, up = gate_up[:, :hidden], gate_up[:, hidden:]
    sigmoid_gate = jax.nn.sigmoid(gate)
    activation = (gate * sigmoid_gate * up).astype(bf16)
    output = vmem_call(
        output_kernel,
        shape(half, width, bf16),
        place, *sum_rows(activation, own_down), middle,
        name="output",
    )

    grad_act = dot(cotangent_all, own_down)
    grad_gate = grad_act * up * sigmoid_gate * (1.0 + gate * (1.0 - sigmoid_gate))
    grad_up = grad_act * gate * sigmoid_gate
    d_gate_up = jnp.concatenate([grad_gate, grad_up], axis=1).astype(bf16)
    grad_middle, branch_own, gain_two_grad = vmem_call(
        back_two_kernel,
        [shape(half, width, f32), shape(half, width, bf16), shape(1, width, f32)],
        place, *sum_rows(d_gate_up, own_gate_up), middle, own_cotangent, own_gains,
        name="back_two",
    )
    d_branch = gather_rows(branch_own)
    grad_down = scatter_grad(cotangent_all, activation, rest)
    grad_gate_up = scatter_grad(normed_two, d_gate_up, rest)

    d_attended = dot(d_branch, own_out).astype(bf16)
    grad_out = scatter_grad(d_branch, attended, rest)
    d_projected, head_grad = attend_back(
        projected,
        d_attended.reshape(2, 4, half, wide_q),
        shift,
        cosine,
        sine,
        head_rows,
        heads_q,
        heads_kv,
    )
    d_projected = d_projected.reshape(-1, wide_qkv)
    input_grad, gain_grads = vmem_call(
        back_one_kernel,
        [shape(half, width, f32), shape(2, width, f32)],
        place, *sum_rows(d_projected, own_qkv), inputs, grad_middle, own_gains, gain_two_grad,
        name="back_one",
    )
    grad_qkv = scatter_grad(normed_one, d_projected, rest)

    sums = jnp.concatenate([gain_grads, head_grad], axis=1)
    for axis in ("c", "x", "y", "zl", "zh"):
        sums = sums + swap(sums, axis)
    if rest > 1:
        sums = lax.psum(sums, "r")
    grad_norm, grad_head = sums[:, :-HEAD_SIZE], sums[:, -HEAD_SIZE:]

    step_value = f32(STEP)

    def step(weight, gradient, first, second):
        return adamw_step(weight.astype(f32), gradient, first, second, step_value, 0.0)

    return (
        output,
        input_grad,
        *adam_qkv(grad_qkv, weight_qkv, first_qkv, second_qkv, wide_q, wide_kv),
        *adam_turned(grad_out, weight_out, first_out, second_out, wide_q),
        *adam_columns(grad_gate_up, weight_gate_up, first_gate_up, second_gate_up, hidden),
        *adam_turned(grad_down, weight_down, first_down, second_down, hidden),
        *step(norm_gains, grad_norm, first_norm, second_norm),
        *step(head_gains, grad_head, first_head, second_head),
    )


def solution(mesh):
    rest = mesh.shape["dp"] // 16
    names = ("zh", "zl", "y", "x", "r", "c")
    cut = Mesh(mesh.devices.reshape(2, 2, 2, 2, rest, 2), names)
    dp = names[:-1]
    rows, tall, wide, copied = P(names, None), P(dp, "c"), P("c", dp), P()
    placed = (rows, rows, tall, wide, tall, wide, copied, copied)
    placed += (tall, tall, wide, wide, tall, tall, wide, wide) + (copied,) * 4
    given = (rows, rows) + (tall,) * 4 + (wide,) * 4 + (tall,) * 4 + (wide,) * 4 + (copied,) * 8
    return jax.shard_map(
        functools.partial(shards, rest),
        mesh=cut,
        in_specs=placed,
        out_specs=given,
        check_vma=False,
    )
```

```python
import functools
import math

import jax
import jax.numpy as jnp
from jax import lax
from jax.experimental import pallas as pl
from jax.experimental.pallas import tpu as pltpu
from jax.sharding import Mesh
from jax.sharding import PartitionSpec as P

HEAD_SIZE = 128
STEP = 10

norm_eps = 1e-06
rope_base = 1000000.0
beta_one = 0.9
beta_two = 0.95
adam_eps = 1e-08
learn_rate = 0.01
weight_decay = 0.1

bf16 = jnp.bfloat16
f32 = jnp.float32

SWAP = [(0, 1), (1, 0)]

FREE = pl.CostEstimate(flops=0, bytes_accessed=0, transcendentals=0)


def dot(left, right):
    return jnp.dot(left, right, preferred_element_type=f32)


def dot_tn(left, right):
    return lax.dot_general(left, right, (((0,), (0,)), ((), ())), preferred_element_type=f32)


def dot_nt(left, right):
    return lax.dot_general(left, right, (((1,), (1,)), ((), ())), preferred_element_type=f32)


def swap(value, axis):
    return lax.ppermute(value, axis, SWAP)


def rms_scale(values):
    return lax.rsqrt(jnp.mean(values * values, axis=-1, keepdims=True) + norm_eps)


def norm_back(upstream, values, scale, gain):
    weighted = upstream * gain
    normed = values * scale
    grad_values = scale * (weighted - normed * jnp.mean(weighted * normed, axis=-1, keepdims=True))
    grad_gain = jnp.sum((upstream * normed).reshape(-1, values.shape[-1]), axis=0)
    return (grad_values, grad_gain)


def adamw_step(weight, gradient, old_first, old_second, step_value, decay):
    moment_one = beta_one * old_first + (1.0 - beta_one) * gradient
    moment_two = beta_two * old_second + (1.0 - beta_two) * gradient * gradient
    fix_one = 1.0 - jnp.power(beta_one, step_value)
    fix_two = 1.0 - jnp.power(beta_two, step_value)
    update = -learn_rate * (
        moment_one / fix_one / (jnp.sqrt(moment_two / fix_two) + adam_eps) + decay * weight
    )
    return (gradient, moment_one, moment_two, update)


def vmem_call(kernel, out_shape, *args, name, flops=0):
    size = sum(math.prod(a.shape) * a.dtype.itemsize for a in (*args, *jax.tree.leaves(out_shape)))
    return pl.pallas_call(
        kernel,
        in_specs=[pl.BlockSpec(memory_space=pltpu.SMEM)] + [pl.BlockSpec(memory_space=pltpu.VMEM)] * (len(args) - 1),
        out_specs=jax.tree.map(lambda _: pl.BlockSpec(memory_space=pltpu.VMEM), out_shape),
        out_shape=out_shape,
        cost_estimate=FREE,
        compiler_params=pltpu.CompilerParams(vmem_limit_bytes=40 * 1024 * 1024),
        name=name,
    )(*args)


def shape(rows, columns, dtype):
    return jax.ShapeDtypeStruct((rows, columns), dtype)


def moves(place_ref, width):
    block = width // 16
    zh, x = place_ref[0], place_ref[1]
    for i in range(16):
        xr, zr, j = i // 8, (i // 4) % 2, i % 4
        natural = ((zr + zh - 2 * zr * zh) * 4 + j) * 2 + (xr + x - 2 * xr * x)
        yield pl.ds(i * block, block), pl.ds(pl.multiple_of(natural * block, block), block)


def start_kernel(place, tokens, cotangent, gains, own_tokens, normed, own_cotangent, own_gains):
    values = tokens[...].astype(f32)
    scale = rms_scale(values)
    for own, natural in moves(place, tokens.shape[1]):
        part = tokens[:, natural]
        gain = gains[:, natural]
        own_tokens[:, own] = part
        own_gains[:, own] = gain
        normed[:, own] = (part.astype(f32) * scale * gain[0:1]).astype(bf16)
        own_cotangent[:, own] = cotangent[:, natural]


def middle_kernel(place, base, near, far, tokens, gains, middle, normed):
    value = tokens[...].astype(f32) + (base[...] + near[...].astype(f32) + far[...].astype(f32))
    middle[...] = value
    normed[...] = (value * rms_scale(value) * gains[1:2]).astype(bf16)


def output_kernel(place, base, near, far, middle, output):
    for own, natural in moves(place, middle.shape[1]):
        added = base[:, own] + near[:, own].astype(f32) + far[:, own].astype(f32)
        output[:, natural] = (middle[:, own] + added).astype(bf16)


def back_two_kernel(place, base, near, far, middle, cotangent, gains, grad_middle, branch, dgain):
    upstream = base[...] + near[...].astype(f32) + far[...].astype(f32)
    value = middle[...]
    part, gain_part = norm_back(upstream, value, rms_scale(value), gains[1:2])
    grad = cotangent[...].astype(f32) + part
    grad_middle[...] = grad
    branch[...] = grad.astype(bf16)
    dgain[...] = gain_part[None]


def back_one_kernel(place, base, near, far, tokens, grad_middle, gains, dgain_two, input_grad, dgain):
    value = tokens[...].astype(f32)
    scale = rms_scale(value)
    upstream = base[...] + near[...].astype(f32) + far[...].astype(f32)
    normed = value * scale
    weighted = upstream * gains[0:1]
    mean = jnp.mean(weighted * normed, axis=-1, keepdims=True)
    for own, natural in moves(place, tokens.shape[1]):
        raised = base[:, own] + near[:, own].astype(f32) + far[:, own].astype(f32)
        unit = tokens[:, own].astype(f32) * scale
        grad = scale * (raised * gains[0:1, own] - unit * mean)
        input_grad[:, natural] = grad_middle[:, own] + grad
        dgain[0:1, natural] = jnp.sum(raised * unit, axis=0, keepdims=True)
        dgain[1:2, natural] = dgain_two[:, own]


def join_kernel(count, *refs):
    parts, out, done = refs[:count], refs[count], refs[count + 1]
    copies, at = [], 0
    for i, part in enumerate(parts):
        rows = part.shape[0]
        copies.append(pltpu.make_async_copy(part, out.at[pl.ds(at, rows)], done.at[i]))
        at += rows
    for copy in copies:
        copy.start()
    for copy in copies:
        copy.wait()


def join(*parts):
    total = shape(sum(p.shape[0] for p in parts), parts[0].shape[1], parts[0].dtype)
    size = 2 * total.shape[0] * total.shape[1] * total.dtype.itemsize
    return pl.pallas_call(
        functools.partial(join_kernel, len(parts)),
        in_specs=[pl.BlockSpec(memory_space=pl.ANY)] * len(parts),
        out_specs=pl.BlockSpec(memory_space=pltpu.VMEM),
        out_shape=total,
        scratch_shapes=[pltpu.SemaphoreType.DMA((len(parts),))],
        cost_estimate=FREE,
        compiler_params=pltpu.CompilerParams(vmem_limit_bytes=16 * 1024 * 1024),
        name="join",
    )(*parts)


def after(value, *others):
    return lax.optimization_barrier((value, *others))[0]


def rows_of(value, count):
    step = value.shape[0] // count
    return [value[i * step : (i + 1) * step] for i in range(count)]


def gather_rows(value, at_send=(), at_half=(), at_whole=()):
    over_zl = swap(value, "zl")
    over_y = swap(value, "y")
    over_both = swap(after(over_zl, *at_send), "y")
    half = join(after(value, *at_half), over_y, over_zl, over_both)
    return join(after(half, *at_whole), swap(half, "c"))


def sum_rows(left, right_t, at_mine=(), at_far=()):
    half = left.shape[0] // 2
    other = swap(dot_nt(left[half:], right_t).astype(bf16), "c")
    mine = dot_nt(left[:half], right_t) + after(other, *at_mine).astype(f32)
    block = rows_of(mine, 4)
    both = swap(block[3].astype(bf16), "y")
    near = swap(block[1].astype(bf16), "y")
    far = swap((block[2] + after(both, *at_far).astype(f32)).astype(bf16), "zl")
    return block[0], near, far


def pack_attention_kernel(wide_q, wide_kv, qkv, out, packed):
    for j in range(4):
        packed[j, :, :wide_q] = qkv[:, j * wide_q : (j + 1) * wide_q]
        for part in range(2):
            at = 4 * (wide_q + part * wide_kv) + j * wide_kv
            to = wide_q + part * wide_kv
            packed[j, :, to : to + wide_kv] = qkv[:, at : at + wide_kv]
        turned = out[j * wide_q : (j + 1) * wide_q, :].astype(f32).T
        packed[j, :, wide_q + 2 * wide_kv :] = turned.astype(bf16)


def pack_attention(qkv, out, wide_q, wide_kv):
    depth = qkv.shape[0]
    packed = jax.ShapeDtypeStruct((4, depth, 2 * wide_q + 2 * wide_kv), bf16)
    return pl.pallas_call(
        functools.partial(pack_attention_kernel, wide_q, wide_kv),
        out_shape=packed,
        cost_estimate=FREE,
        compiler_params=pltpu.CompilerParams(vmem_limit_bytes=40 * 1024 * 1024),
        name="pack_attention",
    )(qkv, out)


def pack_columns_kernel(first, second, packed):
    wide = first.shape[1]
    packed[0, :, :wide] = first[...]
    packed[0, :, wide:] = second[...]


def pack_columns(array, wide):
    depth = array.shape[0]
    return pl.pallas_call(
        pack_columns_kernel,
        grid=(4,),
        in_specs=[
            pl.BlockSpec((depth, wide), lambda j: (0, j)),
            pl.BlockSpec((depth, wide), lambda j: (0, j + 4)),
        ],
        out_specs=pl.BlockSpec((1, depth, 2 * wide), lambda j: (j, 0, 0)),
        out_shape=jax.ShapeDtypeStruct((4, depth, 2 * wide), bf16),
        cost_estimate=FREE,
        compiler_params=pltpu.CompilerParams(vmem_limit_bytes=40 * 1024 * 1024),
        name="pack_columns",
    )(array, array)


def pack_turned_kernel(array, packed):
    packed[0] = array[...].astype(f32).T.astype(bf16)


def pack_turned(array, wide):
    depth = array.shape[1]
    return pl.pallas_call(
        pack_turned_kernel,
        grid=(4,),
        in_specs=[pl.BlockSpec((wide, depth), lambda j: (j, 0))],
        out_specs=pl.BlockSpec((1, depth, wide), lambda j: (j, 0, 0)),
        out_shape=jax.ShapeDtypeStruct((4, depth, wide), bf16),
        cost_estimate=FREE,
        compiler_params=pltpu.CompilerParams(vmem_limit_bytes=40 * 1024 * 1024),
        name="pack_turned",
    )(array)


def exchange(pieces):
    return lax.all_to_all(pieces, ("zl", "y"), 0, 0, tiled=True)


def own_block(pieces, rest):
    mine = exchange(pieces)
    if rest > 1:
        mine = lax.all_gather(mine, "r", axis=1, tiled=True)
    return mine.reshape(-1, mine.shape[-1])


def send_parts(left, right):
    width = left.shape[1]
    part = lambda a, b: dot_tn(left[:, a * width // 4 : b * width // 4], right).astype(bf16)
    return part(3, 4), part(2, 3)


def far_part(left, right, got):
    width = left.shape[1]
    return (dot_tn(left[:, width // 4 : width // 2], right) + got.astype(f32)).astype(bf16)


def own_part(left, right, got, far, rest):
    width = left.shape[1]
    far = jnp.concatenate(far, axis=0).astype(f32)
    mine = dot_tn(left[:, : width // 4], right) + got.astype(f32) + far
    mine = mine.astype(bf16).reshape(4, width // 16, -1)
    if rest > 1:
        mine = lax.psum_scatter(mine, "r", scatter_dimension=1, tiled=True)
    return mine


fix_one = 1.0 - beta_one**STEP
fix_two = 1.0 - beta_two**STEP


def adam_store(refs, at, gradient):
    weight, first, second, grad_out, one_out, two_out, update_out = refs
    moment_one = beta_one * first[at] + (1.0 - beta_one) * gradient
    moment_two = beta_two * second[at] + (1.0 - beta_two) * gradient * gradient
    ratio = moment_one * (1.0 / fix_one) / (jnp.sqrt(moment_two * (1.0 / fix_two)) + adam_eps)
    grad_out[at] = gradient
    one_out[at] = moment_one
    two_out[at] = moment_two
    update_out[at] = -learn_rate * (ratio + weight_decay * weight[at].astype(f32))


def adam_qkv_kernel(wide_q, wide_kv, got, *refs):
    for j in range(4):
        at, to = 0, 0
        for wide in (wide_q, wide_kv, wide_kv):
            part = got[j, :, at : at + wide].astype(f32)
            adam_store(refs, (slice(None), slice(to + j * wide, to + (j + 1) * wide)), part)
            at += wide
            to += 4 * wide


def adam_columns_kernel(got, *refs):
    adam_store(refs, (slice(None), slice(None)), got[0].astype(f32))


def adam_turned_kernel(got, *refs):
    adam_store(refs, (slice(None), slice(None)), got[0].astype(f32).T)


def adam(kernel, grid, got, got_spec, spec, weight, first, second, name):
    out = jax.ShapeDtypeStruct(weight.shape, f32)
    size = math.prod(weight.shape) * 28
    cost = pl.CostEstimate(flops=size // 2, bytes_accessed=size, transcendentals=0)
    return pl.pallas_call(
        kernel,
        grid=grid,
        in_specs=[got_spec, spec, spec, spec],
        out_specs=[spec] * 4,
        out_shape=[out] * 4,
        cost_estimate=cost,
        compiler_params=pltpu.CompilerParams(vmem_limit_bytes=40 * 1024 * 1024),
        name=name,
    )(got, weight, first, second)


def adam_qkv(got, weight, first, second, wide_q, wide_kv):
    kernel = functools.partial(adam_qkv_kernel, wide_q, wide_kv)
    whole = lambda array: pl.BlockSpec(array.shape, lambda i: (0,) * array.ndim)
    return adam(kernel, (1,), got, whole(got), whole(weight), weight, first, second, "adam_qkv")


def adam_columns(got, weight, first, second, wide):
    depth, columns = weight.shape
    got_spec = pl.BlockSpec((1, depth, wide), lambda b: (b % 4, 0, b // 4))
    spec = pl.BlockSpec((depth, wide), lambda b: (0, b))
    grid = (columns // wide,)
    return adam(adam_columns_kernel, grid, got, got_spec, spec, weight, first, second, "adam_columns")


def adam_turned(got, weight, first, second, wide):
    depth = weight.shape[1]
    got_spec = pl.BlockSpec((1, depth, wide), lambda j: (j, 0, 0))
    spec = pl.BlockSpec((wide, depth), lambda j: (j, 0))
    return adam(adam_turned_kernel, (4,), got, got_spec, spec, weight, first, second, "adam_turned")


def rope(v, cosine, sine):
    return v * cosine + pltpu.roll(v, HEAD_SIZE // 2, 1) * sine


def rope_back(v, cosine, sine):
    return v * cosine - pltpu.roll(v, HEAD_SIZE // 2, 1) * sine


def head_norm(v, gain, cosine, sine):
    scale = rms_scale(v)
    return scale, rope(v * scale * gain, cosine, sine).astype(bf16)


def probabilities(q_rot, k_rot, shift):
    length = q_rot.shape[0]
    scores = dot_nt(q_rot, k_rot) * (1.0 / math.sqrt(HEAD_SIZE))
    rows = lax.broadcasted_iota(jnp.int32, (length, length), 0)
    cols = lax.broadcasted_iota(jnp.int32, (length, length), 1)
    place_q = jnp.where(rows >= length - shift, rows + shift - length, rows + shift)
    place_k = jnp.where(cols >= length - shift, cols + shift - length, cols + shift)
    scores = jnp.where(place_q >= place_k, scores, -jnp.inf)
    terms = jnp.exp(scores - jnp.max(scores, axis=-1, keepdims=True))
    return terms / jnp.sum(terms, axis=-1, keepdims=True)


def attend_kernel(heads_q, heads_kv, shift_ref, proj_ref, cos_ref, sin_ref, gain_ref, out_ref):
    half, columns = proj_ref.shape[2:]
    cosine, sine = cos_ref[...], sin_ref[...]
    shift = shift_ref[0]
    group = heads_q // heads_kv

    def column(i):
        return proj_ref[:, 0, :, i * HEAD_SIZE : (i + 1) * HEAD_SIZE].reshape(2 * half, HEAD_SIZE)

    for kv in range(heads_kv):
        _, k_rot = head_norm(column(heads_q + kv), gain_ref[1:2, :], cosine, sine)
        values = column(heads_q + heads_kv + kv).astype(bf16)
        for h in range(kv * group, (kv + 1) * group):
            _, q_rot = head_norm(column(h), gain_ref[0:1, :], cosine, sine)
            probs = probabilities(q_rot, k_rot, shift)
            out = dot(probs.astype(bf16), values).astype(bf16)
            out_ref[:, 0, :, h * HEAD_SIZE : (h + 1) * HEAD_SIZE] = out.reshape(2, half, HEAD_SIZE)


def attend_back_kernel(
    heads_q, heads_kv, shift_ref, proj_ref, datt_ref, cos_ref, sin_ref, gain_ref, out_ref, dgain_ref
):
    half, columns = proj_ref.shape[2:]
    cosine, sine = cos_ref[...], sin_ref[...]
    shift = shift_ref[0]
    group = heads_q // heads_kv
    inv_root = 1.0 / math.sqrt(HEAD_SIZE)

    @pl.when(pl.program_id(0) == 0)
    def _():
        dgain_ref[...] = jnp.zeros_like(dgain_ref)

    def column(ref, i):
        return ref[:, 0, :, i * HEAD_SIZE : (i + 1) * HEAD_SIZE].reshape(2 * half, HEAD_SIZE)

    def store(i, value):
        value = value.astype(bf16).reshape(2, half, HEAD_SIZE)
        out_ref[:, 0, :, i * HEAD_SIZE : (i + 1) * HEAD_SIZE] = value

    q_gain, k_gain = gain_ref[0:1, :], gain_ref[1:2, :]
    dgain_q = jnp.zeros((1, HEAD_SIZE), f32)
    dgain_k = jnp.zeros((1, HEAD_SIZE), f32)
    for kv in range(heads_kv):
        key = column(proj_ref, heads_q + kv)
        k_scale, k_rot = head_norm(key, k_gain, cosine, sine)
        values = column(proj_ref, heads_q + heads_kv + kv).astype(bf16)
        grad_values = jnp.zeros((2 * half, HEAD_SIZE), f32)
        grad_keys = jnp.zeros((2 * half, HEAD_SIZE), f32)
        for h in range(kv * group, (kv + 1) * group):
            query = column(proj_ref, h)
            d_att = column(datt_ref, h)
            q_scale, q_rot = head_norm(query, q_gain, cosine, sine)
            probs = probabilities(q_rot, k_rot, shift)
            grad_probs = dot_nt(d_att, values)
            row_delta = jnp.sum(probs * grad_probs, axis=-1, keepdims=True)
            d_scores = (probs * (grad_probs - row_delta) * inv_root).astype(bf16)
            grad_values += dot_tn(probs.astype(bf16), d_att)
            grad_keys += dot_tn(d_scores, q_rot)
            upstream = rope_back(dot(d_scores, k_rot), cosine, sine)
            raw, gain_part = norm_back(upstream, query, q_scale, q_gain)
            dgain_q += gain_part[None]
            store(h, raw)
        raw, gain_part = norm_back(rope_back(grad_keys, cosine, sine), key, k_scale, k_gain)
        dgain_k += gain_part[None]
        store(heads_q + kv, raw)
        store(heads_q + heads_kv + kv, grad_values)
    dgain_ref[0:1, :] += dgain_q
    dgain_ref[1:2, :] += dgain_k


def block_spec(half, columns):
    return pl.BlockSpec((2, 1, half, columns), lambda s: (0, s, 0, 0))


def whole_spec(array):
    return pl.BlockSpec(array.shape, lambda s: (0,) * array.ndim)


def attend(proj, shift, cosine, sine, gains, heads_q, heads_kv):
    _, seqs, half, columns = proj.shape
    return pl.pallas_call(
        functools.partial(attend_kernel, heads_q, heads_kv),
        grid=(seqs,),
        in_specs=[
            pl.BlockSpec(memory_space=pltpu.SMEM),
            block_spec(half, columns),
            whole_spec(cosine),
            whole_spec(sine),
            whole_spec(gains),
        ],
        out_specs=block_spec(half, heads_q * HEAD_SIZE),
        out_shape=jax.ShapeDtypeStruct((2, seqs, half, heads_q * HEAD_SIZE), bf16),
        cost_estimate=FREE,
        compiler_params=pltpu.CompilerParams(vmem_limit_bytes=32 * 1024 * 1024),
        name="attend",
    )(shift, proj, cosine, sine, gains)


def attend_back(proj, d_att, shift, cosine, sine, gains, heads_q, heads_kv):
    _, seqs, half, columns = proj.shape
    return pl.pallas_call(
        functools.partial(attend_back_kernel, heads_q, heads_kv),
        grid=(seqs,),
        in_specs=[
            pl.BlockSpec(memory_space=pltpu.SMEM),
            block_spec(half, columns),
            block_spec(half, heads_q * HEAD_SIZE),
            whole_spec(cosine),
            whole_spec(sine),
            whole_spec(gains),
        ],
        out_specs=[block_spec(half, columns), pl.BlockSpec((2, HEAD_SIZE), lambda s: (0, 0))],
        out_shape=[
            jax.ShapeDtypeStruct((2, seqs, half, columns), bf16),
            jax.ShapeDtypeStruct((2, HEAD_SIZE), f32),
        ],
        cost_estimate=FREE,
        compiler_params=pltpu.CompilerParams(vmem_limit_bytes=32 * 1024 * 1024),
        name="attend_back",
    )(shift, proj, d_att, cosine, sine, gains)


def shards(
    rest,
    tokens,
    cotangent,
    weight_qkv,
    weight_out,
    weight_gate_up,
    weight_down,
    norm_gains,
    head_gains,
    first_qkv,
    second_qkv,
    first_out,
    second_out,
    first_gate_up,
    second_gate_up,
    first_down,
    second_down,
    first_norm,
    second_norm,
    first_head,
    second_head,
):
    heads_q = weight_out.shape[0] // HEAD_SIZE // 4
    heads_kv = (weight_qkv.shape[1] // HEAD_SIZE - 4 * heads_q) // 2 // 4
    hidden = weight_down.shape[0] // 4
    wide_q, wide_kv = heads_q * HEAD_SIZE, heads_kv * HEAD_SIZE
    wide_qkv = wide_q + 2 * wide_kv
    half, width = tokens.shape
    head_rows = head_gains.astype(f32)
    place = jnp.stack([lax.axis_index("zh"), lax.axis_index("x")]).astype(jnp.int32)

    inputs, normed_own, own_cotangent, own_gains = vmem_call(
        start_kernel,
        [shape(half, width, bf16)] * 3 + [shape(2, width, f32)],
        place, tokens, cotangent, norm_gains.astype(f32),
        name="start",
    )
    together = lax.optimization_barrier
    side = lambda value: swap(value, "x")
    block = own_block(pack_attention(weight_qkv, weight_out, wide_q, wide_kv), rest)
    own, over_zl, over_y = normed_own, swap(normed_own, "zl"), swap(normed_own, "y")
    own, over_zl, over_y, block, packed = together(
        (own, over_zl, over_y, block, pack_columns(weight_gate_up, hidden))
    )
    block_qkv, block_out = block[:, :wide_qkv], block[:, wide_qkv:]
    block_gu = own_block(packed, rest)
    far_qkv, side_qkv, over_both = swap(block_qkv, "zh"), side(block_qkv), swap(over_zl, "y")
    far_qkv, side_qkv, over_both, block_out, packed = together(
        (far_qkv, side_qkv, over_both, block_out, pack_turned(weight_down, hidden))
    )
    both_qkv, far_out, side_out = side(far_qkv), swap(block_out, "zh"), side(block_out)
    half_one = join(own, over_y, over_zl, over_both)
    half_two = swap(half_one, "c")
    both_qkv, far_out, side_out, half_one, half_two, block_gu, packed, own_cotangent = together(
        (both_qkv, far_out, side_out, half_one, half_two, block_gu, packed, own_cotangent)
    )
    normed_one = join(half_one, half_two)
    both_out = side(far_out)
    cotangent_zl, cotangent_y = swap(own_cotangent, "zl"), swap(own_cotangent, "y")
    block_down = own_block(packed, rest)
    side_gu, side_down = side(block_gu), side(block_down)
    far_gu = [swap(part, "zh") for part in rows_of(block_gu, 2)]
    far_down = [swap(block_down, "zh")]
    both_gu = [side(part) for part in far_gu]
    both_down = [side(part) for part in far_down]
    own_qkv = jnp.concatenate([block_qkv, far_qkv, side_qkv, both_qkv], axis=0)
    own_out = jnp.concatenate([block_out, far_out, side_out, both_out], axis=0)
    own_gate_up = jnp.concatenate([block_gu, *far_gu, side_gu, *both_gu], axis=0)
    own_down = jnp.concatenate([block_down, *far_down, side_down, *both_down], axis=0)

    cotangent_both = swap(cotangent_zl, "y")
    cotangent_half = join(own_cotangent, cotangent_y, cotangent_zl, cotangent_both)
    cotangent_all = join(cotangent_half, swap(cotangent_half, "c"))

    core = lax.axis_index("c")
    shift = (core * half).astype(jnp.int32)
    places = (jnp.arange(2 * half) + shift) % (2 * half)
    index = jnp.arange(HEAD_SIZE // 2, dtype=f32)[None, :]
    angles = places.astype(f32)[:, None] * jnp.power(rope_base, -2.0 * index / HEAD_SIZE)
    cosine = jnp.concatenate([jnp.cos(angles)] * 2, axis=1)
    sine = jnp.concatenate([-jnp.sin(angles), jnp.sin(angles)], axis=1)
    shift = shift.reshape(1)

    projected = dot(normed_one, own_qkv)
    projected = projected.reshape(2, 4, half, wide_qkv)
    attended = attend(projected, shift, cosine, sine, head_rows, heads_q, heads_kv)
    attended = after(attended.reshape(-1, wide_q), far_gu[0], cotangent_zl, cotangent_y, block_down)
    middle, normed_own = vmem_call(
        middle_kernel,
        [shape(half, width, f32), shape(half, width, bf16)],
        place,
        *sum_rows(attended, own_out, (cotangent_both,), (far_gu[1], side_gu)),
        inputs, after(own_gains, both_gu[0], cotangent_all),
        name="middle",
    )

    normed_two = gather_rows(
        normed_own, at_send=(*far_down, side_down), at_half=(both_gu[1],)
    )
    gate_up = dot(normed_two, own_gate_up)
    gate, up = gate_up[:, :hidden], gate_up[:, hidden:]
    sigmoid_gate = jax.nn.sigmoid(gate)
    activation = (gate * sigmoid_gate * up).astype(bf16)
    parts = send_parts(cotangent_all, activation)
    grad_act = dot(after(cotangent_all, parts[0]), own_down)
    grad_gate = grad_act * up * sigmoid_gate * (1.0 + gate * (1.0 - sigmoid_gate))
    grad_up = grad_act * gate * sigmoid_gate
    d_gate_up = jnp.concatenate([grad_gate, grad_up], axis=1).astype(bf16)

    side_far, side_near = map(side, parts)
    far = far_part(cotangent_all, activation, side_far)
    far_down = [swap(far, "zh")]
    side_far_gu, side_near_gu = map(side, send_parts(normed_two, d_gate_up))
    far = far_part(normed_two, d_gate_up, side_far_gu)
    far_rows = far
    far_gu = [swap(part, "zh") for part in rows_of(far, 2)]

    grad_middle, branch_own, gain_two_grad = vmem_call(
        back_two_kernel,
        [shape(half, width, f32), shape(half, width, bf16), shape(1, width, f32)],
        place,
        *sum_rows(d_gate_up, own_gate_up, (side_far,), (far_down[0],)),
        middle, own_cotangent, after(own_gains, side_far_gu),
        name="back_two",
    )
    base, near, far = sum_rows(activation, own_down)
    output = vmem_call(
        output_kernel, shape(half, width, bf16), place, base, near, far, middle, name="output"
    )
    d_branch = gather_rows(branch_own, at_send=(far_rows,), at_half=(side_near, far_gu[0]))
    grad_down = exchange(own_part(cotangent_all, activation, side_near, far_down, rest))
    new_down = adam_turned(grad_down, weight_down, first_down, second_down, hidden)

    d_attended = after(dot(d_branch, own_out).astype(bf16), output, grad_down)
    d_projected, head_grad = attend_back(
        projected,
        d_attended.reshape(2, 4, half, wide_q),
        shift,
        cosine,
        sine,
        head_rows,
        heads_q,
        heads_kv,
    )
    d_projected = after(d_projected.reshape(-1, wide_qkv), far_gu[1])
    side_far_out, side_near_out = map(side, send_parts(d_branch, attended))
    far_out = swap(far_part(d_branch, attended, side_far_out), "zh")
    side_far_qkv, side_near_qkv = map(side, send_parts(normed_one, d_projected))
    far_qkv = swap(far_part(normed_one, d_projected, side_far_qkv), "zh")

    grad_gate_up = own_part(normed_two, d_gate_up, side_near_gu, far_gu, rest)
    terms = sum_rows(
        d_projected, own_qkv, at_far=(grad_gate_up, side_far_qkv, side_far_out)
    )
    grad_gate_up = exchange(grad_gate_up)
    new_gate_up = adam_columns(grad_gate_up, weight_gate_up, first_gate_up, second_gate_up, hidden)
    grad_out = exchange(own_part(d_branch, attended, side_near_out, [far_out], rest))
    new_out = adam_turned(grad_out, weight_out, first_out, second_out, wide_q)
    grad_qkv = exchange(own_part(normed_one, d_projected, side_near_qkv, [far_qkv], rest))
    new_qkv = adam_qkv(grad_qkv, weight_qkv, first_qkv, second_qkv, wide_q, wide_kv)
    input_grad, gain_grads = vmem_call(
        back_one_kernel,
        [shape(half, width, f32), shape(2, width, f32)],
        place, *terms, inputs, grad_middle, after(own_gains, far_out, new_down[3]), gain_two_grad,
        name="back_one",
    )

    sums = jnp.concatenate([gain_grads, head_grad], axis=1)
    sums = sums + swap(sums, "c")
    sums = sums + swap(after(sums, new_gate_up[3]), "x")
    sums = sums + swap(after(sums, new_out[3]), "y")
    for axis in ("zl", "zh"):
        sums = sums + swap(sums, axis)
    if rest > 1:
        sums = lax.psum(sums, "r")
    grad_norm, grad_head = sums[:, :-HEAD_SIZE], sums[:, -HEAD_SIZE:]

    step_value = f32(STEP)

    def step(weight, gradient, first, second):
        return adamw_step(weight.astype(f32), gradient, first, second, step_value, 0.0)

    return (
        output,
        input_grad,
        *new_qkv,
        *new_out,
        *new_gate_up,
        *new_down,
        *step(norm_gains, grad_norm, first_norm, second_norm),
        *step(head_gains, grad_head, first_head, second_head),
    )


def solution(mesh):
    rest = mesh.shape["dp"] // 16
    names = ("zh", "zl", "y", "x", "r", "c")
    cut = Mesh(mesh.devices.reshape(2, 2, 2, 2, rest, 2), names)
    dp = names[:-1]
    rows, tall, wide, copied = P(names, None), P(dp, "c"), P("c", dp), P()
    placed = (rows, rows, tall, wide, tall, wide, copied, copied)
    placed += (tall, tall, wide, wide, tall, tall, wide, wide) + (copied,) * 4
    given = (rows, rows) + (tall,) * 4 + (wide,) * 4 + (tall,) * 4 + (wide,) * 4 + (copied,) * 8
    return jax.shard_map(
        functools.partial(shards, rest),
        mesh=cut,
        in_specs=placed,
        out_specs=given,
        check_vma=False,
    )
```

```python
import functools
import math

import jax
import jax.numpy as jnp
from jax import lax
from jax.experimental import pallas as pl
from jax.experimental.pallas import tpu as pltpu
from jax.sharding import Mesh
from jax.sharding import PartitionSpec as P

HEAD_SIZE = 128
STEP = 10

norm_eps = 1e-06
rope_base = 1000000.0
beta_one = 0.9
beta_two = 0.95
adam_eps = 1e-08
learn_rate = 0.01
weight_decay = 0.1

bf16 = jnp.bfloat16
f32 = jnp.float32

SWAP = [(0, 1), (1, 0)]

FREE = pl.CostEstimate(flops=0, bytes_accessed=0, transcendentals=0)


def dot(left, right):
    return jnp.dot(left, right, preferred_element_type=f32)


def dot_tn(left, right):
    return lax.dot_general(left, right, (((0,), (0,)), ((), ())), preferred_element_type=f32)


def dot_nt(left, right):
    return lax.dot_general(left, right, (((1,), (1,)), ((), ())), preferred_element_type=f32)


def swap(value, axis):
    return lax.ppermute(value, axis, SWAP)


def rms_scale(values):
    return lax.rsqrt(jnp.mean(values * values, axis=-1, keepdims=True) + norm_eps)


def norm_back(upstream, values, scale, gain):
    weighted = upstream * gain
    normed = values * scale
    grad_values = scale * (weighted - normed * jnp.mean(weighted * normed, axis=-1, keepdims=True))
    grad_gain = jnp.sum((upstream * normed).reshape(-1, values.shape[-1]), axis=0)
    return (grad_values, grad_gain)


def adamw_step(weight, gradient, old_first, old_second, step_value, decay):
    moment_one = beta_one * old_first + (1.0 - beta_one) * gradient
    moment_two = beta_two * old_second + (1.0 - beta_two) * gradient * gradient
    fix_one = 1.0 - jnp.power(beta_one, step_value)
    fix_two = 1.0 - jnp.power(beta_two, step_value)
    update = -learn_rate * (
        moment_one / fix_one / (jnp.sqrt(moment_two / fix_two) + adam_eps) + decay * weight
    )
    return (gradient, moment_one, moment_two, update)


def vmem_call(kernel, out_shape, *args, name, flops=0):
    size = sum(math.prod(a.shape) * a.dtype.itemsize for a in (*args, *jax.tree.leaves(out_shape)))
    return pl.pallas_call(
        kernel,
        in_specs=[pl.BlockSpec(memory_space=pltpu.SMEM)] + [pl.BlockSpec(memory_space=pltpu.VMEM)] * (len(args) - 1),
        out_specs=jax.tree.map(lambda _: pl.BlockSpec(memory_space=pltpu.VMEM), out_shape),
        out_shape=out_shape,
        cost_estimate=FREE,
        compiler_params=pltpu.CompilerParams(vmem_limit_bytes=40 * 1024 * 1024),
        name=name,
    )(*args)


def shape(rows, columns, dtype):
    return jax.ShapeDtypeStruct((rows, columns), dtype)


def moves(place_ref, width):
    block = width // 16
    zh, x = place_ref[0], place_ref[1]
    for i in range(16):
        xr, zr, j = i // 8, (i // 4) % 2, i % 4
        natural = ((zr + zh - 2 * zr * zh) * 4 + j) * 2 + (xr + x - 2 * xr * x)
        yield pl.ds(i * block, block), pl.ds(pl.multiple_of(natural * block, block), block)


def start_kernel(place, tokens, cotangent, gains, own_tokens, normed, own_cotangent, own_gains):
    values = tokens[...].astype(f32)
    scale = rms_scale(values)
    for own, natural in moves(place, tokens.shape[1]):
        part = tokens[:, natural]
        gain = gains[:, natural]
        own_tokens[:, own] = part
        own_gains[:, own] = gain
        normed[:, own] = (part.astype(f32) * scale * gain[0:1]).astype(bf16)
        own_cotangent[:, own] = cotangent[:, natural]


def middle_kernel(place, base, near, far, tokens, gains, middle, normed):
    value = tokens[...].astype(f32) + (base[...] + near[...].astype(f32) + far[...].astype(f32))
    middle[...] = value
    normed[...] = (value * rms_scale(value) * gains[1:2]).astype(bf16)


def output_kernel(place, base, near, far, middle, output):
    for own, natural in moves(place, middle.shape[1]):
        added = base[:, own] + near[:, own].astype(f32) + far[:, own].astype(f32)
        output[:, natural] = (middle[:, own] + added).astype(bf16)


def back_two_kernel(place, base, near, far, middle, cotangent, gains, grad_middle, branch, dgain):
    upstream = base[...] + near[...].astype(f32) + far[...].astype(f32)
    value = middle[...]
    part, gain_part = norm_back(upstream, value, rms_scale(value), gains[1:2])
    grad = cotangent[...].astype(f32) + part
    grad_middle[...] = grad
    branch[...] = grad.astype(bf16)
    dgain[...] = gain_part[None]


def back_one_kernel(place, base, near, far, tokens, grad_middle, gains, dgain_two, input_grad, dgain):
    value = tokens[...].astype(f32)
    scale = rms_scale(value)
    upstream = base[...] + near[...].astype(f32) + far[...].astype(f32)
    normed = value * scale
    weighted = upstream * gains[0:1]
    mean = jnp.mean(weighted * normed, axis=-1, keepdims=True)
    for own, natural in moves(place, tokens.shape[1]):
        raised = base[:, own] + near[:, own].astype(f32) + far[:, own].astype(f32)
        unit = tokens[:, own].astype(f32) * scale
        grad = scale * (raised * gains[0:1, own] - unit * mean)
        input_grad[:, natural] = grad_middle[:, own] + grad
        dgain[0:1, natural] = jnp.sum(raised * unit, axis=0, keepdims=True)
        dgain[1:2, natural] = dgain_two[:, own]


def join_kernel(count, *refs):
    parts, out, done = refs[:count], refs[count], refs[count + 1]
    copies, at = [], 0
    for i, part in enumerate(parts):
        rows = part.shape[0]
        copies.append(pltpu.make_async_copy(part, out.at[pl.ds(at, rows)], done.at[i]))
        at += rows
    for copy in copies:
        copy.start()
    for copy in copies:
        copy.wait()


def join(*parts):
    total = shape(sum(p.shape[0] for p in parts), parts[0].shape[1], parts[0].dtype)
    size = 2 * total.shape[0] * total.shape[1] * total.dtype.itemsize
    return pl.pallas_call(
        functools.partial(join_kernel, len(parts)),
        in_specs=[pl.BlockSpec(memory_space=pl.ANY)] * len(parts),
        out_specs=pl.BlockSpec(memory_space=pltpu.VMEM),
        out_shape=total,
        scratch_shapes=[pltpu.SemaphoreType.DMA((len(parts),))],
        cost_estimate=FREE,
        compiler_params=pltpu.CompilerParams(vmem_limit_bytes=16 * 1024 * 1024),
        name="join",
    )(*parts)


def after(value, *others):
    return lax.optimization_barrier((value, *others))[0]


def rows_of(value, count):
    step = value.shape[0] // count
    return [value[i * step : (i + 1) * step] for i in range(count)]


def gather_rows(value, at_send=(), at_half=(), at_whole=()):
    over_zl = swap(value, "zl")
    over_y = swap(value, "y")
    over_both = swap(after(over_zl, *at_send), "y")
    half = join(after(value, *at_half), over_y, over_zl, over_both)
    return join(after(half, *at_whole), swap(half, "c"))


def sum_cores(left, right_t, at_mine=None):
    half = left.shape[0] // 2
    other = swap(dot_nt(left[half:], right_t).astype(bf16), "c")
    if at_mine is not None:
        other = after(other, *at_mine)
    return dot_nt(left[:half], right_t) + other.astype(f32)


def sum_chips(mine, at_far=None):
    block = rows_of(mine, 4)
    both, near = swap(block[3].astype(bf16), "y"), swap(block[1].astype(bf16), "y")
    came = both if at_far is None else after(both, *at_far)
    return block[0], near, swap((block[2] + came.astype(f32)).astype(bf16), "zl"), both


def pack_attention_kernel(wide_q, wide_kv, qkv, out, packed):
    for j in range(4):
        packed[j, :, :wide_q] = qkv[:, j * wide_q : (j + 1) * wide_q]
        for part in range(2):
            at = 4 * (wide_q + part * wide_kv) + j * wide_kv
            to = wide_q + part * wide_kv
            packed[j, :, to : to + wide_kv] = qkv[:, at : at + wide_kv]
        turned = out[j * wide_q : (j + 1) * wide_q, :].astype(f32).T
        packed[j, :, wide_q + 2 * wide_kv :] = turned.astype(bf16)


def pack_attention(qkv, out, wide_q, wide_kv):
    depth = qkv.shape[0]
    packed = jax.ShapeDtypeStruct((4, depth, 2 * wide_q + 2 * wide_kv), bf16)
    return pl.pallas_call(
        functools.partial(pack_attention_kernel, wide_q, wide_kv),
        out_shape=packed,
        cost_estimate=FREE,
        compiler_params=pltpu.CompilerParams(vmem_limit_bytes=40 * 1024 * 1024),
        name="pack_attention",
    )(qkv, out)


def pack_columns_kernel(first, second, packed):
    wide = first.shape[1]
    packed[0, :, :wide] = first[...]
    packed[0, :, wide:] = second[...]


def pack_columns(array, wide):
    depth = array.shape[0]
    return pl.pallas_call(
        pack_columns_kernel,
        grid=(4,),
        in_specs=[
            pl.BlockSpec((depth, wide), lambda j: (0, j)),
            pl.BlockSpec((depth, wide), lambda j: (0, j + 4)),
        ],
        out_specs=pl.BlockSpec((1, depth, 2 * wide), lambda j: (j, 0, 0)),
        out_shape=jax.ShapeDtypeStruct((4, depth, 2 * wide), bf16),
        cost_estimate=FREE,
        compiler_params=pltpu.CompilerParams(vmem_limit_bytes=40 * 1024 * 1024),
        name="pack_columns",
    )(array, array)


def pack_turned_kernel(array, packed):
    packed[0] = array[...].astype(f32).T.astype(bf16)


def pack_turned(array, wide):
    depth = array.shape[1]
    return pl.pallas_call(
        pack_turned_kernel,
        grid=(4,),
        in_specs=[pl.BlockSpec((wide, depth), lambda j: (j, 0))],
        out_specs=pl.BlockSpec((1, depth, wide), lambda j: (j, 0, 0)),
        out_shape=jax.ShapeDtypeStruct((4, depth, wide), bf16),
        cost_estimate=FREE,
        compiler_params=pltpu.CompilerParams(vmem_limit_bytes=40 * 1024 * 1024),
        name="pack_turned",
    )(array)


def exchange(pieces):
    return lax.all_to_all(pieces, ("zl", "y"), 0, 0, tiled=True)


def own_block(pieces, rest):
    mine = exchange(pieces)
    if rest > 1:
        mine = lax.all_gather(mine, "r", axis=1, tiled=True)
    return mine.reshape(-1, mine.shape[-1])


def send_parts(left, right):
    width = left.shape[1]
    part = lambda a, b: dot_tn(left[:, a * width // 4 : b * width // 4], right).astype(bf16)
    return part(3, 4), part(2, 3)


def far_part(left, right, got):
    width = left.shape[1]
    return (dot_tn(left[:, width // 4 : width // 2], right) + got.astype(f32)).astype(bf16)


def own_part(left, right, got, far, rest):
    width = left.shape[1]
    far = jnp.concatenate(far, axis=0).astype(f32)
    mine = dot_tn(left[:, : width // 4], right) + got.astype(f32) + far
    mine = mine.astype(bf16).reshape(4, width // 16, -1)
    if rest > 1:
        mine = lax.psum_scatter(mine, "r", scatter_dimension=1, tiled=True)
    return mine


fix_one = 1.0 - beta_one**STEP
fix_two = 1.0 - beta_two**STEP


def adam_store(refs, at, gradient):
    weight, first, second, grad_out, one_out, two_out, update_out = refs
    moment_one = beta_one * first[at] + (1.0 - beta_one) * gradient
    moment_two = beta_two * second[at] + (1.0 - beta_two) * gradient * gradient
    ratio = moment_one * (1.0 / fix_one) / (jnp.sqrt(moment_two * (1.0 / fix_two)) + adam_eps)
    grad_out[at] = gradient
    one_out[at] = moment_one
    two_out[at] = moment_two
    update_out[at] = -learn_rate * (ratio + weight_decay * weight[at].astype(f32))


def adam_qkv_kernel(wide_q, wide_kv, got, *refs):
    for j in range(4):
        at, to = 0, 0
        for wide in (wide_q, wide_kv, wide_kv):
            part = got[j, :, at : at + wide].astype(f32)
            adam_store(refs, (slice(None), slice(to + j * wide, to + (j + 1) * wide)), part)
            at += wide
            to += 4 * wide


def adam_columns_kernel(got, *refs):
    adam_store(refs, (slice(None), slice(None)), got[0].astype(f32))


def adam_turned_kernel(got, *refs):
    adam_store(refs, (slice(None), slice(None)), got[0].astype(f32).T)


def adam(kernel, grid, got, got_spec, spec, weight, first, second, name):
    out = jax.ShapeDtypeStruct(weight.shape, f32)
    size = math.prod(weight.shape) * 28
    cost = pl.CostEstimate(flops=size // 2, bytes_accessed=size, transcendentals=0)
    return pl.pallas_call(
        kernel,
        grid=grid,
        in_specs=[got_spec, spec, spec, spec],
        out_specs=[spec] * 4,
        out_shape=[out] * 4,
        cost_estimate=cost,
        compiler_params=pltpu.CompilerParams(vmem_limit_bytes=40 * 1024 * 1024),
        name=name,
    )(got, weight, first, second)


def adam_qkv(got, weight, first, second, wide_q, wide_kv):
    kernel = functools.partial(adam_qkv_kernel, wide_q, wide_kv)
    whole = lambda array: pl.BlockSpec(array.shape, lambda i: (0,) * array.ndim)
    return adam(kernel, (1,), got, whole(got), whole(weight), weight, first, second, "adam_qkv")


def adam_columns(got, weight, first, second, wide):
    depth, columns = weight.shape
    got_spec = pl.BlockSpec((1, depth, wide), lambda b: (b % 4, 0, b // 4))
    spec = pl.BlockSpec((depth, wide), lambda b: (0, b))
    grid = (columns // wide,)
    return adam(adam_columns_kernel, grid, got, got_spec, spec, weight, first, second, "adam_columns")


def adam_turned(got, weight, first, second, wide):
    depth = weight.shape[1]
    got_spec = pl.BlockSpec((1, depth, wide), lambda j: (j, 0, 0))
    spec = pl.BlockSpec((wide, depth), lambda j: (j, 0))
    return adam(adam_turned_kernel, (4,), got, got_spec, spec, weight, first, second, "adam_turned")


def rope(v, cosine, sine):
    return v * cosine + pltpu.roll(v, HEAD_SIZE // 2, 1) * sine


def rope_back(v, cosine, sine):
    return v * cosine - pltpu.roll(v, HEAD_SIZE // 2, 1) * sine


def head_norm(v, gain, cosine, sine):
    scale = rms_scale(v)
    return scale, rope(v * scale * gain, cosine, sine).astype(bf16)


def probabilities(q_rot, k_rot, shift):
    length = q_rot.shape[0]
    scores = dot_nt(q_rot, k_rot) * (1.0 / math.sqrt(HEAD_SIZE))
    rows = lax.broadcasted_iota(jnp.int32, (length, length), 0)
    cols = lax.broadcasted_iota(jnp.int32, (length, length), 1)
    place_q = jnp.where(rows >= length - shift, rows + shift - length, rows + shift)
    place_k = jnp.where(cols >= length - shift, cols + shift - length, cols + shift)
    scores = jnp.where(place_q >= place_k, scores, -jnp.inf)
    terms = jnp.exp(scores - jnp.max(scores, axis=-1, keepdims=True))
    return terms / jnp.sum(terms, axis=-1, keepdims=True)


def attend_kernel(heads_q, heads_kv, shift_ref, proj_ref, cos_ref, sin_ref, gain_ref, out_ref):
    half, columns = proj_ref.shape[2:]
    cosine, sine = cos_ref[...], sin_ref[...]
    shift = shift_ref[0]
    group = heads_q // heads_kv

    def column(i):
        return proj_ref[:, 0, :, i * HEAD_SIZE : (i + 1) * HEAD_SIZE].reshape(2 * half, HEAD_SIZE)

    for kv in range(heads_kv):
        _, k_rot = head_norm(column(heads_q + kv), gain_ref[1:2, :], cosine, sine)
        values = column(heads_q + heads_kv + kv).astype(bf16)
        for h in range(kv * group, (kv + 1) * group):
            _, q_rot = head_norm(column(h), gain_ref[0:1, :], cosine, sine)
            probs = probabilities(q_rot, k_rot, shift)
            out = dot(probs.astype(bf16), values).astype(bf16)
            out_ref[:, 0, :, h * HEAD_SIZE : (h + 1) * HEAD_SIZE] = out.reshape(2, half, HEAD_SIZE)


def attend_back_kernel(
    heads_q, heads_kv, shift_ref, proj_ref, datt_ref, cos_ref, sin_ref, gain_ref, out_ref, dgain_ref
):
    half, columns = proj_ref.shape[2:]
    cosine, sine = cos_ref[...], sin_ref[...]
    shift = shift_ref[0]
    group = heads_q // heads_kv
    inv_root = 1.0 / math.sqrt(HEAD_SIZE)

    @pl.when(pl.program_id(0) == 0)
    def _():
        dgain_ref[...] = jnp.zeros_like(dgain_ref)

    def column(ref, i):
        return ref[:, 0, :, i * HEAD_SIZE : (i + 1) * HEAD_SIZE].reshape(2 * half, HEAD_SIZE)

    def store(i, value):
        value = value.astype(bf16).reshape(2, half, HEAD_SIZE)
        out_ref[:, 0, :, i * HEAD_SIZE : (i + 1) * HEAD_SIZE] = value

    q_gain, k_gain = gain_ref[0:1, :], gain_ref[1:2, :]
    dgain_q = jnp.zeros((1, HEAD_SIZE), f32)
    dgain_k = jnp.zeros((1, HEAD_SIZE), f32)
    for kv in range(heads_kv):
        key = column(proj_ref, heads_q + kv)
        k_scale, k_rot = head_norm(key, k_gain, cosine, sine)
        values = column(proj_ref, heads_q + heads_kv + kv).astype(bf16)
        grad_values = jnp.zeros((2 * half, HEAD_SIZE), f32)
        grad_keys = jnp.zeros((2 * half, HEAD_SIZE), f32)
        for h in range(kv * group, (kv + 1) * group):
            query = column(proj_ref, h)
            d_att = column(datt_ref, h)
            q_scale, q_rot = head_norm(query, q_gain, cosine, sine)
            probs = probabilities(q_rot, k_rot, shift)
            grad_probs = dot_nt(d_att, values)
            row_delta = jnp.sum(probs * grad_probs, axis=-1, keepdims=True)
            d_scores = (probs * (grad_probs - row_delta) * inv_root).astype(bf16)
            grad_values += dot_tn(probs.astype(bf16), d_att)
            grad_keys += dot_tn(d_scores, q_rot)
            upstream = rope_back(dot(d_scores, k_rot), cosine, sine)
            raw, gain_part = norm_back(upstream, query, q_scale, q_gain)
            dgain_q += gain_part[None]
            store(h, raw)
        raw, gain_part = norm_back(rope_back(grad_keys, cosine, sine), key, k_scale, k_gain)
        dgain_k += gain_part[None]
        store(heads_q + kv, raw)
        store(heads_q + heads_kv + kv, grad_values)
    dgain_ref[0:1, :] += dgain_q
    dgain_ref[1:2, :] += dgain_k


def block_spec(half, columns):
    return pl.BlockSpec((2, 1, half, columns), lambda s: (0, s, 0, 0))


def whole_spec(array):
    return pl.BlockSpec(array.shape, lambda s: (0,) * array.ndim)


def attend(proj, shift, cosine, sine, gains, heads_q, heads_kv):
    _, seqs, half, columns = proj.shape
    return pl.pallas_call(
        functools.partial(attend_kernel, heads_q, heads_kv),
        grid=(seqs,),
        in_specs=[
            pl.BlockSpec(memory_space=pltpu.SMEM),
            block_spec(half, columns),
            whole_spec(cosine),
            whole_spec(sine),
            whole_spec(gains),
        ],
        out_specs=block_spec(half, heads_q * HEAD_SIZE),
        out_shape=jax.ShapeDtypeStruct((2, seqs, half, heads_q * HEAD_SIZE), bf16),
        cost_estimate=FREE,
        compiler_params=pltpu.CompilerParams(vmem_limit_bytes=32 * 1024 * 1024),
        name="attend",
    )(shift, proj, cosine, sine, gains)


def attend_back(proj, d_att, shift, cosine, sine, gains, heads_q, heads_kv):
    _, seqs, half, columns = proj.shape
    return pl.pallas_call(
        functools.partial(attend_back_kernel, heads_q, heads_kv),
        grid=(seqs,),
        in_specs=[
            pl.BlockSpec(memory_space=pltpu.SMEM),
            block_spec(half, columns),
            block_spec(half, heads_q * HEAD_SIZE),
            whole_spec(cosine),
            whole_spec(sine),
            whole_spec(gains),
        ],
        out_specs=[block_spec(half, columns), pl.BlockSpec((2, HEAD_SIZE), lambda s: (0, 0))],
        out_shape=[
            jax.ShapeDtypeStruct((2, seqs, half, columns), bf16),
            jax.ShapeDtypeStruct((2, HEAD_SIZE), f32),
        ],
        cost_estimate=FREE,
        compiler_params=pltpu.CompilerParams(vmem_limit_bytes=32 * 1024 * 1024),
        name="attend_back",
    )(shift, proj, d_att, cosine, sine, gains)


def shards(
    rest,
    tokens,
    cotangent,
    weight_qkv,
    weight_out,
    weight_gate_up,
    weight_down,
    norm_gains,
    head_gains,
    first_qkv,
    second_qkv,
    first_out,
    second_out,
    first_gate_up,
    second_gate_up,
    first_down,
    second_down,
    first_norm,
    second_norm,
    first_head,
    second_head,
):
    heads_q = weight_out.shape[0] // HEAD_SIZE // 4
    heads_kv = (weight_qkv.shape[1] // HEAD_SIZE - 4 * heads_q) // 2 // 4
    hidden = weight_down.shape[0] // 4
    wide_q, wide_kv = heads_q * HEAD_SIZE, heads_kv * HEAD_SIZE
    wide_qkv = wide_q + 2 * wide_kv
    half, width = tokens.shape
    head_rows = head_gains.astype(f32)
    place = jnp.stack([lax.axis_index("zh"), lax.axis_index("x")]).astype(jnp.int32)

    inputs, normed_own, own_cotangent, own_gains = vmem_call(
        start_kernel,
        [shape(half, width, bf16)] * 3 + [shape(2, width, f32)],
        place, tokens, cotangent, norm_gains.astype(f32),
        name="start",
    )
    together = lax.optimization_barrier
    side = lambda value: swap(value, "x")
    block = own_block(pack_attention(weight_qkv, weight_out, wide_q, wide_kv), rest)
    own, over_zl, over_y = normed_own, swap(normed_own, "zl"), swap(normed_own, "y")
    own, over_zl, over_y, block, packed = together(
        (own, over_zl, over_y, block, pack_columns(weight_gate_up, hidden))
    )
    block_qkv, block_out = block[:, :wide_qkv], block[:, wide_qkv:]
    block_gu = own_block(packed, rest)
    far_qkv, side_qkv, over_both = swap(block_qkv, "zh"), side(block_qkv), swap(over_zl, "y")
    far_qkv, side_qkv, over_both, block_out, packed = together(
        (far_qkv, side_qkv, over_both, block_out, pack_turned(weight_down, hidden))
    )
    both_qkv, far_out, side_out = side(far_qkv), swap(block_out, "zh"), side(block_out)
    half_one = join(own, over_y, over_zl, over_both)
    half_two = swap(half_one, "c")
    both_qkv, far_out, side_out, half_one, half_two, block_gu, packed, own_cotangent = together(
        (both_qkv, far_out, side_out, half_one, half_two, block_gu, packed, own_cotangent)
    )
    normed_one = join(half_one, half_two)
    both_out = side(far_out)
    cotangent_zl, cotangent_y = swap(own_cotangent, "zl"), swap(own_cotangent, "y")
    block_down = own_block(packed, rest)
    side_gu, side_down = side(block_gu), side(block_down)
    far_gu = [swap(part, "zh") for part in rows_of(block_gu, 2)]
    far_down = [swap(block_down, "zh")]
    both_gu = [side(part) for part in far_gu]
    both_down = [side(part) for part in far_down]
    own_qkv = jnp.concatenate([block_qkv, far_qkv, side_qkv, both_qkv], axis=0)
    own_out = jnp.concatenate([block_out, far_out, side_out, both_out], axis=0)
    own_gate_up = jnp.concatenate([block_gu, *far_gu, side_gu, *both_gu], axis=0)
    own_down = jnp.concatenate([block_down, *far_down, side_down, *both_down], axis=0)

    cotangent_both = swap(cotangent_zl, "y")
    cotangent_half = join(own_cotangent, cotangent_y, cotangent_zl, cotangent_both)
    cotangent_all = join(cotangent_half, swap(cotangent_half, "c"))

    core = lax.axis_index("c")
    shift = (core * half).astype(jnp.int32)
    places = (jnp.arange(2 * half) + shift) % (2 * half)
    index = jnp.arange(HEAD_SIZE // 2, dtype=f32)[None, :]
    angles = places.astype(f32)[:, None] * jnp.power(rope_base, -2.0 * index / HEAD_SIZE)
    cosine = jnp.concatenate([jnp.cos(angles)] * 2, axis=1)
    sine = jnp.concatenate([-jnp.sin(angles), jnp.sin(angles)], axis=1)
    shift = shift.reshape(1)

    projected = dot(normed_one, own_qkv)
    projected = projected.reshape(2, 4, half, wide_qkv)
    attended = attend(projected, shift, cosine, sine, head_rows, heads_q, heads_kv)
    attended = after(
        attended.reshape(-1, wide_q), block_down, cotangent_zl, cotangent_y, far_gu[0]
    )
    mine = sum_cores(attended, own_out, (cotangent_both,))
    terms = sum_chips(mine, (side_gu, far_gu[1]))[:3]
    middle, normed_own = vmem_call(
        middle_kernel,
        [shape(half, width, f32), shape(half, width, bf16)],
        place, *terms, inputs, after(own_gains, cotangent_all),
        name="middle",
    )
    normed_two = gather_rows(normed_own, (side_down,), (*both_gu, *far_down))
    gate_up = dot(normed_two, own_gate_up)
    gate, up = gate_up[:, :hidden], gate_up[:, hidden:]
    sigmoid_gate = jax.nn.sigmoid(gate)
    activation = (gate * sigmoid_gate * up).astype(bf16)
    parts = send_parts(cotangent_all, activation)
    grad_act = dot(after(cotangent_all, parts[0]), own_down)
    grad_gate = grad_act * up * sigmoid_gate * (1.0 + gate * (1.0 - sigmoid_gate))
    grad_up = grad_act * gate * sigmoid_gate
    d_gate_up = jnp.concatenate([grad_gate, grad_up], axis=1).astype(bf16)

    side_far, side_near = map(side, parts)
    far = far_part(cotangent_all, activation, side_far)
    far_down = [swap(part, "zh") for part in rows_of(far, 2)]
    side_far_gu, side_near_gu = map(side, send_parts(normed_two, d_gate_up))
    far_rows = far_part(normed_two, d_gate_up, side_far_gu)
    far_gu = [swap(part, "zh") for part in rows_of(far_rows, 2)]
    grad_down = own_part(cotangent_all, activation, side_near, far_down, rest)
    got_down = exchange(grad_down)
    new_down = adam_turned(got_down, weight_down, first_down, second_down, hidden)
    own_sum_gu = own_part(normed_two, d_gate_up, side_near_gu, far_gu, rest)
    grad_gate_up = exchange(own_sum_gu)
    new_gate_up = adam_columns(grad_gate_up, weight_gate_up, first_gate_up, second_gate_up, hidden)
    mine = sum_cores(activation, own_down)
    base, near_output, far_output, _ = sum_chips(mine)
    output = vmem_call(
        output_kernel, shape(half, width, bf16), place, base, near_output, far_output, middle, name="output"
    )

    terms = sum_chips(sum_cores(d_gate_up, own_gate_up, (side_far,)), far_down)[:3]
    grad_middle, branch_own, gain_two_grad = vmem_call(
        back_two_kernel,
        [shape(half, width, f32), shape(half, width, bf16), shape(1, width, f32)],
        place, *terms, middle, own_cotangent, after(own_gains, side_far_gu),
        name="back_two",
    )
    d_branch = gather_rows(branch_own, (far_rows,), (side_near, far_gu[0]), (near_output,))
    side_far_out, side_near_out = map(side, send_parts(d_branch, attended))
    far_out = far_part(d_branch, attended, side_far_out)
    far_out = swap(far_out, "zh")
    grad_out = exchange(own_part(d_branch, attended, side_near_out, [far_out], rest))
    new_out = adam_turned(grad_out, weight_out, first_out, second_out, wide_q)

    d_attended = after(dot(d_branch, own_out).astype(bf16), new_down[3])
    d_projected, head_grad = attend_back(
        projected,
        d_attended.reshape(2, 4, half, wide_q),
        shift,
        cosine,
        sine,
        head_rows,
        heads_q,
        heads_kv,
    )
    d_projected = after(d_projected.reshape(-1, wide_qkv), got_down, far_output)
    side_far_qkv, side_near_qkv = map(side, send_parts(normed_one, d_projected))
    far_qkv = far_part(normed_one, d_projected, side_far_qkv)
    far_qkv = swap(far_qkv, "zh")
    grad_qkv = exchange(own_part(normed_one, d_projected, side_near_qkv, [far_qkv], rest))
    new_qkv = adam_qkv(grad_qkv, weight_qkv, first_qkv, second_qkv, wide_q, wide_kv)
    terms = sum_chips(sum_cores(d_projected, own_qkv, ()), (far_gu[1], side_far_qkv))[:3]
    back_one_gains = after(own_gains, own_sum_gu, side_far_out, side_near_out, far_out)
    input_grad, gain_grads = vmem_call(
        back_one_kernel,
        [shape(half, width, f32), shape(2, width, f32)],
        place, *terms, inputs, grad_middle, back_one_gains, gain_two_grad,
        name="back_one",
    )

    sums = jnp.concatenate([gain_grads, head_grad], axis=1)
    steps = (("c", new_gate_up[3:]), ("x", ()), ("y", ()), ("zl", new_out[3:]), ("zh", ()))
    for axis, ready in steps:
        sums = after(sums, *ready)
        sums = sums + swap(sums, axis)
    if rest > 1:
        sums = lax.psum(sums, "r")
    grad_norm, grad_head = sums[:, :-HEAD_SIZE], sums[:, -HEAD_SIZE:]

    step_value = f32(STEP)

    def step(weight, gradient, first, second):
        return adamw_step(weight.astype(f32), gradient, first, second, step_value, 0.0)

    return (
        output,
        input_grad,
        *new_qkv,
        *new_out,
        *new_gate_up,
        *new_down,
        *step(norm_gains, grad_norm, first_norm, second_norm),
        *step(head_gains, grad_head, first_head, second_head),
    )


def solution(mesh):
    rest = mesh.shape["dp"] // 16
    names = ("zh", "zl", "y", "x", "r", "c")
    cut = Mesh(mesh.devices.reshape(2, 2, 2, 2, rest, 2), names)
    dp = names[:-1]
    rows, tall, wide, copied = P(names, None), P(dp, "c"), P("c", dp), P()
    placed = (rows, rows, tall, wide, tall, wide, copied, copied)
    placed += (tall, tall, wide, wide, tall, tall, wide, wide) + (copied,) * 4
    given = (rows, rows) + (tall,) * 4 + (wide,) * 4 + (tall,) * 4 + (wide,) * 4 + (copied,) * 8
    return jax.shard_map(
        functools.partial(shards, rest),
        mesh=cut,
        in_specs=placed,
        out_specs=given,
        check_vma=False,
    )
```
